32 devices in a mesh: groups: 2 (over y), samples: 8 (over z, x), terms: 2 (over core).
Axes of the slice: x: 2, y: 2, z: 4, core: 2. Of those that a mesh axis runs over, the one named last changes fastest.
Arguments:
- sample_points: float32 [8192, 10], P(('groups', 'samples')), parts along dimension 0, may hold values from -1 to 1
- observed: float32 [8192, 48], P(('groups', 'samples')), parts along dimension 0, may hold values from -60 to 60
- multi_index: int32 [8008, 10], replicated, may hold values from 0 to 6, as said below
Outputs:
- coefficients: float32 [16016, 48], P(('groups', 'terms')), parts along dimension 0
- left_vectors: float32 [8192, 48], P(('groups', 'samples')), parts along dimension 0
The draws below stay inside these ranges and needn't reach their ends.
There are 2 independent parts, one for each index of `groups`. The reference program is written for one: setup_inputs(seed, part) draws one part's arguments, and reference() takes and returns one part's arrays. A program takes and returns all parts, laid end to end along the dimension named above; an argument that names none is the same for every part. Nothing has to cross between parts.
Inputs may be any that keep to these rules, and one draw needn't show every extreme that they name: `multi_index`: each row holds the degrees of the 10 inputs in one basis term; the rows are all multi-indices of total degree at most 6, each once, in some order.
All inputs are finite; a program needn't handle non-finite values.
Results may differ from the reference program's by a relative error of at most 0.0052.
Values sent between devices are 32-bit elements; how exact they have to be, the bound alone decides.
A program may use at most 64 MiB of HBM per device.

```python
import math
import jax
import jax.numpy as jnp
import numpy as np
from jax import lax

INPUTS = 10
DEGREE = 6
TERMS = 8008
FIELDS = 48
ITERS = 2
SAMPLES = 4096


def degree_table():
    prefixes = [[]]
    for column in range(INPUTS):
        extended = []
        for prefix in prefixes:
            used_degree = sum(prefix)
            for order in range(DEGREE + 1 - used_degree):
                extended.append(prefix + [order])
        prefixes = extended
    return np.array(prefixes, dtype=np.int32)


def draw_multi_index(key, part):
    table = jnp.asarray(degree_table())
    row_order = jax.random.permutation(key, TERMS)
    column_order = jax.random.permutation(jax.random.fold_in(key, 1), INPUTS)
    return table[row_order][:, column_order].astype(jnp.int32)


def draw_observed(key, part):
    keys = jax.random.split(jax.random.fold_in(key, 7), 2)
    position = jnp.arange(SAMPLES, dtype=jnp.float32)
    rising = 1.0 + 2.0 * position / max(SAMPLES - 1, 1)
    column_scale = jnp.exp(jax.random.uniform(keys[1], (FIELDS,), jnp.float32, math.log(0.5), math.log(4.0)))
    base = jnp.clip(jax.random.normal(keys[0], (SAMPLES, FIELDS), jnp.float32), -5.0, 5.0)
    return (base * rising[:, None] * column_scale[None, :]).astype(jnp.float32)


def level_of(rng, extent, cuts, least, largest):
    factor_of, own = 1.0, jax.random.fold_in(rng, 6)
    for axis_at, parts in cuts:
        heights = jnp.exp(jax.random.uniform(jax.random.fold_in(own, axis_at), (parts,), jnp.float32, least / len(cuts), largest / len(cuts)))
        factor_of = factor_of * jnp.repeat(heights, extent[axis_at] // parts).reshape([-1 if axis == axis_at else 1 for axis in range(len(extent))])
    return factor_of


def setup_inputs(seed: int = 0, part: int = 0) -> dict:
    splits = jax.random.split(jax.random.key(seed), 4)
    part_keys = jax.random.split(jax.random.fold_in(splits[3], part), 4)
    return {
        "sample_points": jnp.clip(jax.random.uniform(part_keys[0], (SAMPLES, INPUTS), jnp.float32, -1.0, 1.0) * level_of(part_keys[0], (SAMPLES, INPUTS), ((0, 8),), -0.4, 0.0), -1.0, 1.0),
        "observed": draw_observed(jax.random.fold_in(jax.random.fold_in(splits[3], part), 71), part),
        "multi_index": draw_multi_index(jax.random.fold_in(splits[3], 71), part),
    }


EPS = 1e-06

def legendre(points):
    values = [jnp.ones_like(points), points]
    for order in range(1, DEGREE):
        values.append(((2 * order + 1) * points * values[order] - order * values[order - 1]) / (order + 1))
    values = values[:DEGREE + 1]
    factors = jnp.sqrt(jnp.arange(DEGREE + 1, dtype=jnp.float32) * 2 + 1)
    return jnp.stack(values, axis=-1) * factors

def pair_values(points):
    values = legendre(points)
    code_width = (DEGREE + 1) ** 2
    joined = values[:, 0::2, :, None] * values[:, 1::2, None, :]
    return joined.reshape(points.shape[0], points.shape[1] // 2, code_width)

def transposed(design, left_rows):
    return lax.dot_general(design.astype(jnp.float32), left_rows.astype(jnp.float32), (((0,), (0,)), ((), ())), precision=lax.Precision.HIGHEST, preferred_element_type=jnp.float32)

def reference(sample_points, observed, multi_index):
    pair_count = INPUTS // 2
    codes = jnp.stack([multi_index[:, 2 * pair_index] * (DEGREE + 1) + multi_index[:, 2 * pair_index + 1] for pair_index in range(pair_count)]).astype(jnp.int32)
    block_rows = math.gcd(SAMPLES, 1024)
    block_count = SAMPLES // block_rows
    inverse_root = 1.0 / math.sqrt(SAMPLES)

    def build_block(points):
        pair_table = pair_values(points)
        product = jnp.ones((points.shape[0], TERMS), jnp.float32)
        for pair_index in range(pair_count):
            product = product * jnp.take(pair_table[:, pair_index, :], codes[pair_index], axis=1)
        return product
    point_blocks = sample_points.reshape(block_count, block_rows, INPUTS)
    field_blocks = observed.reshape(block_count, block_rows, FIELDS)

    def first_sweep(carry, block):
        points, values = block
        product = build_block(points)
        squares = lax.optimization_barrier(jnp.sum(product * product, axis=1))
        weights = jnp.sqrt(TERMS / squares)
        row_scale = weights * inverse_root
        rhs = weights[:, None] * values
        design = product.astype(jnp.bfloat16)
        total_sq, total_terms = carry
        total_sq = total_sq + lax.optimization_barrier(jnp.sum(rhs * rhs, axis=0))
        total_terms = total_terms + transposed(design, (row_scale[:, None] * rhs).astype(jnp.bfloat16))
        return ((total_sq, total_terms), (row_scale, rhs))
    start = (jnp.zeros((FIELDS,), jnp.float32), jnp.zeros((TERMS, FIELDS), jnp.float32))
    (sumsq, term_sum), (scale_blocks, rhs_blocks) = lax.scan(first_sweep, start, (point_blocks, field_blocks))
    beta_now = jnp.sqrt(sumsq + EPS)
    left_blocks = rhs_blocks / beta_now
    raw = term_sum / beta_now
    alpha_now = jnp.sqrt(lax.optimization_barrier(jnp.sum(raw * raw, axis=0)) + EPS)
    right_vec = raw / alpha_now
    direction = right_vec
    coeffs = jnp.zeros((TERMS, FIELDS), jnp.float32)
    phibar = beta_now
    rhobar = alpha_now
    for iteration in range(ITERS):

        def sweep(carry, block, right_vec=right_vec, alpha_now=alpha_now):
            points, row_scale, left_rows = block
            design = build_block(points).astype(jnp.bfloat16)
            rounded_right = right_vec.astype(jnp.bfloat16).astype(jnp.float32)
            image = jnp.dot(design.astype(jnp.float32), rounded_right, precision=lax.Precision.HIGHEST, preferred_element_type=jnp.float32)
            partial_value = row_scale[:, None] * image - alpha_now * left_rows
            total_sq, total_terms = carry
            total_sq = total_sq + lax.optimization_barrier(jnp.sum(partial_value * partial_value, axis=0))
            total_terms = total_terms + transposed(design, (row_scale[:, None] * partial_value).astype(jnp.bfloat16))
            return ((total_sq, total_terms), partial_value)
        (sumsq, term_sum), partial_blocks = lax.scan(sweep, start, (point_blocks, scale_blocks, left_blocks))
        beta_now = jnp.sqrt(sumsq + EPS)
        left_blocks = partial_blocks / beta_now
        raw = term_sum / beta_now - beta_now * right_vec
        alpha_now = jnp.sqrt(lax.optimization_barrier(jnp.sum(raw * raw, axis=0)) + EPS)
        right_vec = raw / alpha_now
        rho_val = jnp.sqrt(rhobar * rhobar + beta_now * beta_now)
        cosine = rhobar / rho_val
        sine = beta_now / rho_val
        theta_val = sine * alpha_now
        rhobar = -cosine * alpha_now
        phi_val = cosine * phibar
        phibar = sine * phibar
        coeffs = coeffs + phi_val / rho_val * direction
        direction = right_vec - theta_val / rho_val * direction
    return (coeffs, left_blocks.reshape(SAMPLES, FIELDS))
```

```python
import functools
import itertools
import math

import jax
import jax.numpy as jnp
import numpy as np
from jax import lax
from jax.experimental import pallas as pl
from jax.experimental.pallas import tpu as pltpu
from jax.sharding import PartitionSpec as P

INPUTS = 10
DEGREE = 6
TERMS = 8008
FIELDS = 48
EPS = 1e-06
MESH = pl.DeviceIdType.MESH

GROUPS = (((0, 1, 2), 256), ((3, 4, 5), 256), ((6, 7), 128), ((8, 9), 128))
PAD_INPUTS = 16
PIECES = 3


def group_codes(count):
    return [c for c in itertools.product(range(DEGREE + 1), repeat=count) if sum(c) <= DEGREE]


def code_key(code):
    return sum(int(d) * (DEGREE + 1) ** i for i, d in enumerate(code))


def constants():
    depth = (DEGREE + 1) * PIECES * PAD_INPUTS
    blocks = []
    keys = np.full((8, 256), -2, np.int32)
    for g, (inputs, width) in enumerate(GROUPS):
        codes = group_codes(len(inputs)) * PIECES
        for r, code in enumerate(codes):
            keys[g, r] = code_key(code)
        for i, source in enumerate(inputs):
            block = np.zeros((width, depth), np.float32)
            for r, code in enumerate(codes):
                for piece in range(PIECES):
                    block[r, (code[i] * PIECES + piece) * PAD_INPUTS + source] = 1.0
            blocks.append(block)
    return np.concatenate(blocks), keys


def pieces_of(value):
    high = value.astype(jnp.bfloat16).astype(jnp.float32)
    rest = value - high
    middle = rest.astype(jnp.bfloat16).astype(jnp.float32)
    return high, middle, rest - middle


def fit_kernel(
    n, width, share, inverse_root,
    points_ref, observed_ref, keys_ref, picks_ref, entries_ref,
    coeffs_ref, left_ref,
    design, t0, t1, t2, t3, send1, recv1, all1, send2, recv2, all2, cross_out, cross_in, norm_out, norm_in, total_in,
    rs_send, rs_recv, ag_send, ag_recv, cross_send, cross_recv, norm_send, norm_recv, tot_send, tot_recv,
):
    me = lax.axis_index("samples")
    core = lax.axis_index("terms")
    rows = points_ref.shape[1]
    tables = (t0, t1, t2, t3)

    barrier = pltpu.get_barrier_semaphore()

    def greet(step, _):
        pl.semaphore_signal(barrier, inc=1, device_id={"samples": lax.rem(me + step, n)}, device_id_type=MESH)
        return 0

    lax.fori_loop(1, n, greet, 0)
    pl.semaphore_signal(barrier, inc=1, device_id={"terms": 1 - core}, device_id_type=MESH)
    pl.semaphore_wait(barrier, n)

    x = points_ref[...]
    values = [jnp.ones_like(x), x]
    for order in range(1, DEGREE):
        values.append(
            ((2 * order + 1) * x * values[order] - order * values[order - 1]) / (order + 1)
        )
    values = [v * np.float32(math.sqrt(2 * k + 1)) for k, v in enumerate(values)]
    parts = []
    for v in values:
        parts.extend(p.astype(jnp.bfloat16) for p in pieces_of(v))
    flat = jnp.concatenate(parts, axis=0)

    offset = 0
    for g, (inputs, table_width) in enumerate(GROUPS):
        table = None
        for _ in inputs:
            factor = jnp.dot(
                picks_ref[offset:offset + table_width, :], flat, preferred_element_type=jnp.float32
            )
            table = factor if table is None else table * factor
            offset += table_width
        count = len(group_codes(len(inputs)))
        row = lax.broadcasted_iota(jnp.int32, table.shape, 0)
        high, middle, low = pieces_of(table)
        tables[g][...] = jnp.where(
            row < count, high, jnp.where(row < 2 * count, middle, low)
        ).astype(jnp.bfloat16)

    squared = [v * v for v in values]
    poly = [squared[k][0:1, :] for k in range(DEGREE + 1)]
    for j in range(1, INPUTS):
        own = [squared[k][j:j + 1, :] for k in range(DEGREE + 1)]
        fresh = []
        for d in range(DEGREE + 1):
            total = poly[d] * own[0]
            for k in range(1, d + 1):
                total = total + poly[d - k] * own[k]
            fresh.append(total)
        poly = fresh
    squares = functools.reduce(lambda a, b: a + b, poly)
    weights = jnp.sqrt(TERMS / squares)
    row_scale = weights * np.float32(inverse_root)
    rhs = weights * observed_ref[...]

    lane = lax.broadcasted_iota(jnp.int32, (FIELDS, width), 1)
    last = lane == width - 1

    def row_sums(value):
        return jnp.sum(value * value, axis=1, keepdims=True)

    def remote(src, dst, send_sem, recv_sem, peer):
        return pltpu.make_async_remote_copy(
            src_ref=src, dst_ref=dst, send_sem=send_sem, recv_sem=recv_sem,
            device_id=peer, device_id_type=MESH,
        )

    tile = min(width, 256)

    def build_chunk(q):
        def build_tile(i, _):
            at = pl.multiple_of(q * width + i * tile, tile)
            keys = keys_ref[pl.ds(at, tile), :]
            product = None
            for g, (_, table_width) in enumerate(GROUPS):
                hot = jnp.where(
                    keys[:, g:g + 1] == entries_ref[g:g + 1, 0:table_width], 1.0, 0.0
                ).astype(jnp.bfloat16)
                picked = jnp.dot(hot, tables[g][...], preferred_element_type=jnp.float32)
                product = picked if product is None else product * picked
            design[pl.ds(at, tile), :] = product.astype(jnp.bfloat16)
            return 0

        lax.fori_loop(0, width // tile, build_tile, 0)

    def transposed_all(left_rows, norm, phase, send, recv, build):
        left_cast = left_rows.astype(jnp.bfloat16)

        def one(step, _):
            q = lax.rem(me + step, n)
            if build:
                build_chunk(q)
            at = pl.multiple_of(q * width, width)
            chunk = lax.dot_general(
                left_cast, design[pl.ds(at, width), :], (((1,), (1,)), ((), ())),
                preferred_element_type=jnp.float32,
            )
            chunk = jnp.where(last, norm, chunk)

            @pl.when(step < n)
            def _():
                send[q] = chunk
                remote(
                    send.at[q], recv.at[me], rs_send.at[phase, q], rs_recv.at[phase, me], {"samples": q}
                ).start()

            @pl.when(step == n)
            def _():
                recv[me] = chunk

            return 0

        lax.fori_loop(1, n + 1, one, 0)

        def arrived(step, _):
            q = lax.rem(me + step, n)
            copy = remote(
                send.at[q], recv.at[q], rs_send.at[phase, q], rs_recv.at[phase, q], {"samples": q}
            )
            copy.wait_recv()
            copy.wait_send()
            return 0

        lax.fori_loop(1, n, arrived, 0)
        return lax.fori_loop(0, n, lambda q, acc: acc + recv[q], jnp.zeros((FIELDS, width), jnp.float32))

    def gather(mine, phase, blocks):
        blocks[me] = mine

        def start(step, _):
            q = lax.rem(me + step, n)
            remote(
                blocks.at[me], blocks.at[me], ag_send.at[phase, q], ag_recv.at[phase, me], {"samples": q}
            ).start()
            return 0

        def finish(step, _):
            q = lax.rem(me + step, n)
            copy = remote(
                blocks.at[me], blocks.at[q], ag_send.at[phase, q], ag_recv.at[phase, q], {"samples": q}
            )
            copy.wait_recv()
            copy.wait_send()
            return 0

        lax.fori_loop(1, n, start, 0)
        lax.fori_loop(1, n, finish, 0)

    def term_norm(phase, blocks):
        half = lax.fori_loop(
            0, n, lambda q, acc: acc + blocks[q][:, width - 1:width], jnp.zeros((FIELDS, 1), jnp.float32)
        )
        norm_out[phase] = jnp.broadcast_to(half, (FIELDS, 128))
        copy = remote(
            norm_out.at[phase], norm_in.at[phase], norm_send.at[phase], norm_recv.at[phase], {"terms": 1 - core}
        )
        copy.start()
        copy.wait()
        return jnp.sqrt(half + norm_in[phase][:, 0:1] + EPS)

    def row_product(phase, blocks, alpha):
        def one(q, acc):
            right = blocks[q] / alpha
            blocks[q] = right
            at = pl.multiple_of(q * width, width)
            return acc + jnp.dot(
                right.astype(jnp.bfloat16), design[pl.ds(at, width), :], preferred_element_type=jnp.float32
            )

        mine = lax.fori_loop(0, n, one, jnp.zeros((FIELDS, rows), jnp.float32))
        cross_out[phase] = mine
        copy = remote(
            cross_out.at[phase], cross_in.at[phase], cross_send.at[phase], cross_recv.at[phase], {"terms": 1 - core}
        )
        copy.start()
        copy.wait()
        return mine + cross_in[phase]

    summed = transposed_all(row_scale * rhs, row_sums(rhs), 0, send1, recv1, True)
    beta = jnp.sqrt(summed[:, width - 1:width] + EPS)
    left = rhs / beta
    raw = jnp.where(last, 0.0, summed) / beta
    gather(jnp.where(last, row_sums(raw), raw), 0, all1)
    alpha = term_norm(0, all1)
    phibar = beta
    rhobar = alpha

    partial = row_scale * row_product(0, all1, alpha) - alpha * left
    summed = transposed_all(row_scale * partial, row_sums(partial), 1, send2, recv2, False)
    beta = jnp.sqrt(summed[:, width - 1:width] + EPS)
    left = partial / beta
    raw = jnp.where(last, 0.0, summed / beta - beta * all1[me])
    gather(jnp.where(last, row_sums(raw), raw), 1, all2)
    alpha = term_norm(1, all2)
    rho = jnp.sqrt(rhobar * rhobar + beta * beta)
    cosine = rhobar / rho
    sine = beta / rho
    theta = sine * alpha
    rhobar = -cosine * alpha
    first = cosine * phibar / rho
    turn = theta / rho
    phibar = sine * phibar

    partial = row_scale * row_product(1, all2, alpha) - alpha * left
    total_in[me] = jnp.broadcast_to(row_sums(partial), (FIELDS, 128))

    def start_total(step, _):
        q = lax.rem(me + step, n)
        remote(total_in.at[me], total_in.at[me], tot_send.at[q], tot_recv.at[me], {"samples": q}).start()
        return 0

    def finish_total(step, _):
        q = lax.rem(me + step, n)
        copy = remote(total_in.at[me], total_in.at[q], tot_send.at[q], tot_recv.at[q], {"samples": q})
        copy.wait_recv()
        copy.wait_send()
        return 0

    lax.fori_loop(1, n, start_total, 0)
    lax.fori_loop(1, n, finish_total, 0)
    square = lax.fori_loop(
        0, n, lambda q, acc: acc + total_in[q][:, 0:1], jnp.zeros((FIELDS, 1), jnp.float32)
    )
    beta = jnp.sqrt(square + EPS)
    left_ref[...] = partial / beta
    rho = jnp.sqrt(rhobar * rhobar + beta * beta)
    second = rhobar / rho * phibar / rho

    def combine(q, _):
        direction = all1[q]
        coeffs_ref[q] = first * direction + second * (all2[q] - turn * direction)
        return 0

    lax.fori_loop(0, n, combine, 0)


def per_device(sample_points, observed, multi_index):
    n = lax.axis_size("samples")
    cores = lax.axis_size("terms")
    rows = sample_points.shape[0]
    inverse_root = 1.0 / math.sqrt(rows * n)
    share = TERMS // cores
    held = -(-share // n)
    width = -(-(held + 1) // 128) * 128
    picks, entries = constants()

    my_terms = lax.dynamic_slice_in_dim(multi_index, lax.axis_index("terms") * share, share, 0)
    powers = np.zeros((INPUTS, 8), np.int32)
    for g, (inputs, _) in enumerate(GROUPS):
        for i, source in enumerate(inputs):
            powers[source, g] = (DEGREE + 1) ** i
    keys = jnp.sum(my_terms[:, :, None] * powers[None], axis=1)
    keys = jnp.pad(keys, ((0, held * n - share), (0, 0)), constant_values=-1)
    keys = jnp.pad(keys.reshape(n, held, 8), ((0, 0), (0, width - held), (0, 0)), constant_values=-1)
    keys = keys.reshape(n * width, 8)
    points = jnp.pad(sample_points.T, ((0, PAD_INPUTS - INPUTS), (0, 0)))

    blocks = (n, FIELDS, width)
    vmem = pl.BlockSpec(memory_space=pltpu.VMEM)
    dma = pltpu.SemaphoreType.DMA
    f32 = jnp.float32
    coeffs, left = pl.pallas_call(
        functools.partial(fit_kernel, n, width, share, inverse_root),
        out_shape=(
            jax.ShapeDtypeStruct(blocks, f32),
            jax.ShapeDtypeStruct((FIELDS, rows), f32),
        ),
        in_specs=[vmem] * 5,
        out_specs=(vmem, vmem),
        scratch_shapes=[
            pltpu.VMEM((n * width, rows), jnp.bfloat16),
            *(pltpu.VMEM((table_width, rows), jnp.bfloat16) for _, table_width in GROUPS),
            *(pltpu.VMEM(blocks, f32) for _ in range(6)),
            pltpu.VMEM((2, FIELDS, rows), f32),
            pltpu.VMEM((2, FIELDS, rows), f32),
            pltpu.VMEM((2, FIELDS, 128), f32),
            pltpu.VMEM((2, FIELDS, 128), f32),
            pltpu.VMEM((n, FIELDS, 128), f32),
            dma((2, n)), dma((2, n)), dma((2, n)), dma((2, n)),
            dma((2,)), dma((2,)), dma((2,)), dma((2,)),
            dma((n,)), dma((n,)),
        ],
        compiler_params=pltpu.CompilerParams(
            collective_id=0, has_side_effects=True, vmem_limit_bytes=48 * 1024 * 1024
        ),
    )(points, observed.T, keys, jnp.asarray(picks, jnp.bfloat16), jnp.asarray(entries))
    coeffs = coeffs.transpose(0, 2, 1)[:, :held, :].reshape(held * n, FIELDS)[:share]
    return coeffs, left.T


def solution(mesh):
    in_specs = (P(("groups", "samples"), None), P(("groups", "samples"), None), P())
    out_specs = (P(("groups", "terms"), None), P(("groups", "samples"), None))
    return jax.shard_map(
        per_device, mesh=mesh, in_specs=in_specs, out_specs=out_specs, check_vma=False
    )
```

```python
import functools
import itertools
import math

import jax
import jax.numpy as jnp
import numpy as np
from jax import lax
from jax.experimental import pallas as pl
from jax.experimental.pallas import tpu as pltpu
from jax.sharding import PartitionSpec as P

INPUTS = 10
DEGREE = 6
TERMS = 8008
FIELDS = 48
EPS = 1e-06
MESH = pl.DeviceIdType.MESH

GROUPS = (((0, 1, 2), 256), ((3, 4, 5), 256), ((6, 7), 128), ((8, 9), 128))
PAD_INPUTS = 16
PIECES = 3


def group_codes(count):
    return [c for c in itertools.product(range(DEGREE + 1), repeat=count) if sum(c) <= DEGREE]


def code_key(code):
    return sum(int(d) * (DEGREE + 1) ** i for i, d in enumerate(code))


def constants():
    depth = (DEGREE + 1) * PIECES * PAD_INPUTS
    blocks = []
    keys = np.full((8, 256), -2, np.int32)
    for g, (inputs, width) in enumerate(GROUPS):
        codes = group_codes(len(inputs)) * PIECES
        for r, code in enumerate(codes):
            keys[g, r] = code_key(code)
        for i, source in enumerate(inputs):
            block = np.zeros((width, depth), np.float32)
            for r, code in enumerate(codes):
                for piece in range(PIECES):
                    block[r, (code[i] * PIECES + piece) * PAD_INPUTS + source] = 1.0
            blocks.append(block)
    return np.concatenate(blocks), keys


def pieces_of(value):
    high = value.astype(jnp.bfloat16).astype(jnp.float32)
    rest = value - high
    middle = rest.astype(jnp.bfloat16).astype(jnp.float32)
    return high, middle, rest - middle


def fit_kernel(
    n, width, share, inverse_root,
    points_ref, observed_ref, keys_ref, picks_ref, entries_ref,
    coeffs_ref, left_ref,
    design, t0, t1, t2, t3, send1, met1, recv1, all1, send2, met2, recv2, all2, cross_out, cross_in, norm_out, norm_in, total_in,
    pair_send, pair_recv, rs_send, rs_recv, ag_send, fw_send, ag_recv, cross_send, cross_recv, norm_send, norm_recv, tot_send, tot_recv,
):
    me = lax.axis_index("samples")
    core = lax.axis_index("terms")
    rows = points_ref.shape[1]
    tables = (t0, t1, t2, t3)

    barrier = pltpu.get_barrier_semaphore()

    def greet(step, _):
        pl.semaphore_signal(barrier, inc=1, device_id={"samples": lax.rem(me + step, n)}, device_id_type=MESH)
        return 0

    lax.fori_loop(1, n, greet, 0)
    pl.semaphore_signal(barrier, inc=1, device_id={"terms": 1 - core}, device_id_type=MESH)
    pl.semaphore_wait(barrier, n)

    x = points_ref[...]
    values = [jnp.ones_like(x), x]
    for order in range(1, DEGREE):
        values.append(
            ((2 * order + 1) * x * values[order] - order * values[order - 1]) / (order + 1)
        )
    values = [v * np.float32(math.sqrt(2 * k + 1)) for k, v in enumerate(values)]
    parts = []
    for v in values:
        parts.extend(p.astype(jnp.bfloat16) for p in pieces_of(v))
    flat = jnp.concatenate(parts, axis=0)

    offset = 0
    for g, (inputs, table_width) in enumerate(GROUPS):
        table = None
        for _ in inputs:
            factor = jnp.dot(
                picks_ref[offset:offset + table_width, :], flat, preferred_element_type=jnp.float32
            )
            table = factor if table is None else table * factor
            offset += table_width
        count = len(group_codes(len(inputs)))
        row = lax.broadcasted_iota(jnp.int32, table.shape, 0)
        high, middle, low = pieces_of(table)
        tables[g][...] = jnp.where(
            row < count, high, jnp.where(row < 2 * count, middle, low)
        ).astype(jnp.bfloat16)

    squared = [v * v for v in values]
    poly = [squared[k][0:1, :] for k in range(DEGREE + 1)]
    for j in range(1, INPUTS):
        own = [squared[k][j:j + 1, :] for k in range(DEGREE + 1)]
        fresh = []
        for d in range(DEGREE + 1):
            total = poly[d] * own[0]
            for k in range(1, d + 1):
                total = total + poly[d - k] * own[k]
            fresh.append(total)
        poly = fresh
    squares = functools.reduce(lambda a, b: a + b, poly)
    weights = jnp.sqrt(TERMS / squares)
    row_scale = weights * np.float32(inverse_root)
    rhs = weights * observed_ref[...]

    lane = lax.broadcasted_iota(jnp.int32, (FIELDS, width), 1)
    last = lane == width - 1

    def row_sums(value):
        return jnp.sum(value * value, axis=1, keepdims=True)

    def remote(src, dst, send_sem, recv_sem, peer):
        return pltpu.make_async_remote_copy(
            src_ref=src, dst_ref=dst, send_sem=send_sem, recv_sem=recv_sem,
            device_id=peer, device_id_type=MESH,
        )

    tile = min(width, 256)

    def build_chunk(q):
        def build_tile(i, _):
            at = pl.multiple_of(q * width + i * tile, tile)
            keys = keys_ref[pl.ds(at, tile), :]
            product = None
            for g, (_, table_width) in enumerate(GROUPS):
                hot = jnp.where(
                    keys[:, g:g + 1] == entries_ref[g:g + 1, 0:table_width], 1.0, 0.0
                ).astype(jnp.bfloat16)
                picked = jnp.dot(hot, tables[g][...], preferred_element_type=jnp.float32)
                product = picked if product is None else product * picked
            design[pl.ds(at, tile), :] = product.astype(jnp.bfloat16)
            return 0

        lax.fori_loop(0, width // tile, build_tile, 0)

    half = n // 2
    mine_h = me // 2
    mine_p = lax.rem(me, 2)
    across = 2 * mine_h + 1 - mine_p

    def transposed_all(left_rows, norm, phase, send, met, recv, build):
        left_cast = left_rows.astype(jnp.bfloat16)

        def partial_chunk(q):
            if build:
                build_chunk(q)
            at = pl.multiple_of(q * width, width)
            chunk = lax.dot_general(
                left_cast, design[pl.ds(at, width), :], (((1,), (1,)), ((), ())),
                preferred_element_type=jnp.float32,
            )
            return jnp.where(last, norm, chunk)

        def pair_copy(h):
            return remote(
                send.at[2 * h + 1 - mine_p], met.at[h],
                pair_send.at[phase, h], pair_recv.at[phase, h], {"samples": across},
            )

        def to_pair(step, _):
            h = lax.rem(mine_h + step, half)
            send[2 * h + 1 - mine_p] = partial_chunk(2 * h + 1 - mine_p)
            pair_copy(h).start()
            return 0

        lax.fori_loop(1, half + 1, to_pair, 0)

        def to_owner(step, _):
            h = lax.rem(mine_h + step, half)
            q = 2 * h + mine_p
            chunk = partial_chunk(q)
            pair_copy(h).wait_recv()
            chunk = chunk + met[h]

            @pl.when(step < half)
            def _():
                send[q] = chunk
                remote(
                    send.at[q], recv.at[mine_h], rs_send.at[phase, h], rs_recv.at[phase, mine_h], {"samples": q}
                ).start()

            @pl.when(step == half)
            def _():
                recv[mine_h] = chunk

            return 0

        lax.fori_loop(1, half + 1, to_owner, 0)

        def arrived(step, _):
            h = lax.rem(mine_h + step, half)
            q = 2 * h + mine_p
            copy = remote(
                send.at[q], recv.at[h], rs_send.at[phase, h], rs_recv.at[phase, h], {"samples": q}
            )
            copy.wait_recv()
            copy.wait_send()
            return 0

        def pair_sent(h, _):
            pair_copy(h).wait_send()
            return 0

        lax.fori_loop(1, half, arrived, 0)
        lax.fori_loop(0, half, pair_sent, 0)
        return lax.fori_loop(0, half, lambda h, acc: acc + recv[h], jnp.zeros((FIELDS, width), jnp.float32))

    def gather(mine, phase, blocks):
        blocks[me] = mine

        def forward(h):
            q = 2 * h + mine_p
            return remote(
                blocks.at[q], blocks.at[q], fw_send.at[phase, h], ag_recv.at[phase, q], {"samples": across}
            )

        def spread(h, slot):
            return remote(
                blocks.at[me], blocks.at[slot], ag_send.at[phase, h], ag_recv.at[phase, slot],
                {"samples": 2 * h + mine_p},
            )

        def start(step, _):
            spread(lax.rem(mine_h + step, half), me).start()
            return 0

        def hand_on(step, _):
            h = lax.rem(mine_h + half - step, half)
            spread(h, 2 * h + mine_p).wait_recv()
            forward(h).start()
            return 0

        def finish(h, _):
            q = 2 * h + 1 - mine_p
            remote(
                blocks.at[q], blocks.at[q], fw_send.at[phase, h], ag_recv.at[phase, q], {"samples": across}
            ).wait_recv()
            forward(h).wait_send()
            return 0

        def sent(step, _):
            spread(lax.rem(mine_h + step, half), me).wait_send()
            return 0

        forward(mine_h).start()
        lax.fori_loop(1, half, start, 0)
        lax.fori_loop(1, half, hand_on, 0)
        lax.fori_loop(0, half, finish, 0)
        lax.fori_loop(1, half, sent, 0)

    def term_norm(phase, blocks):
        square = lax.fori_loop(
            0, n, lambda q, acc: acc + blocks[q][:, width - 1:width], jnp.zeros((FIELDS, 1), jnp.float32)
        )
        norm_out[phase] = jnp.broadcast_to(square, (FIELDS, 128))
        copy = remote(
            norm_out.at[phase], norm_in.at[phase], norm_send.at[phase], norm_recv.at[phase], {"terms": 1 - core}
        )
        copy.start()
        copy.wait()
        return jnp.sqrt(square + norm_in[phase][:, 0:1] + EPS)

    def row_product(phase, blocks, alpha):
        def one(q, acc):
            right = blocks[q] / alpha
            blocks[q] = right
            at = pl.multiple_of(q * width, width)
            return acc + jnp.dot(
                right.astype(jnp.bfloat16), design[pl.ds(at, width), :], preferred_element_type=jnp.float32
            )

        mine = lax.fori_loop(0, n, one, jnp.zeros((FIELDS, rows), jnp.float32))
        cross_out[phase] = mine
        copy = remote(
            cross_out.at[phase], cross_in.at[phase], cross_send.at[phase], cross_recv.at[phase], {"terms": 1 - core}
        )
        copy.start()
        copy.wait()
        return mine + cross_in[phase]

    summed = transposed_all(row_scale * rhs, row_sums(rhs), 0, send1, met1, recv1, True)
    beta = jnp.sqrt(summed[:, width - 1:width] + EPS)
    left = rhs / beta
    raw = jnp.where(last, 0.0, summed) / beta
    gather(jnp.where(last, row_sums(raw), raw), 0, all1)
    alpha = term_norm(0, all1)
    phibar = beta
    rhobar = alpha

    partial = row_scale * row_product(0, all1, alpha) - alpha * left
    summed = transposed_all(row_scale * partial, row_sums(partial), 1, send2, met2, recv2, False)
    beta = jnp.sqrt(summed[:, width - 1:width] + EPS)
    left = partial / beta
    raw = jnp.where(last, 0.0, summed / beta - beta * all1[me])
    gather(jnp.where(last, row_sums(raw), raw), 1, all2)
    alpha = term_norm(1, all2)
    rho = jnp.sqrt(rhobar * rhobar + beta * beta)
    cosine = rhobar / rho
    sine = beta / rho
    theta = sine * alpha
    rhobar = -cosine * alpha
    first = cosine * phibar / rho
    turn = theta / rho
    phibar = sine * phibar

    partial = row_scale * row_product(1, all2, alpha) - alpha * left
    total_in[me] = jnp.broadcast_to(row_sums(partial), (FIELDS, 128))

    def start_total(step, _):
        q = lax.rem(me + step, n)
        remote(total_in.at[me], total_in.at[me], tot_send.at[q], tot_recv.at[me], {"samples": q}).start()
        return 0

    def finish_total(step, _):
        q = lax.rem(me + step, n)
        copy = remote(total_in.at[me], total_in.at[q], tot_send.at[q], tot_recv.at[q], {"samples": q})
        copy.wait_recv()
        copy.wait_send()
        return 0

    lax.fori_loop(1, n, start_total, 0)
    lax.fori_loop(1, n, finish_total, 0)
    square = lax.fori_loop(
        0, n, lambda q, acc: acc + total_in[q][:, 0:1], jnp.zeros((FIELDS, 1), jnp.float32)
    )
    beta = jnp.sqrt(square + EPS)
    left_ref[...] = partial / beta
    rho = jnp.sqrt(rhobar * rhobar + beta * beta)
    second = rhobar / rho * phibar / rho

    def combine(q, _):
        direction = all1[q]
        coeffs_ref[q] = first * direction + second * (all2[q] - turn * direction)
        return 0

    lax.fori_loop(0, n, combine, 0)


def per_device(sample_points, observed, multi_index):
    n = lax.axis_size("samples")
    cores = lax.axis_size("terms")
    rows = sample_points.shape[0]
    inverse_root = 1.0 / math.sqrt(rows * n)
    share = TERMS // cores
    held = -(-share // n)
    width = -(-(held + 1) // 128) * 128
    picks, entries = constants()

    my_terms = lax.dynamic_slice_in_dim(multi_index, lax.axis_index("terms") * share, share, 0)
    powers = np.zeros((INPUTS, 8), np.int32)
    for g, (inputs, _) in enumerate(GROUPS):
        for i, source in enumerate(inputs):
            powers[source, g] = (DEGREE + 1) ** i
    keys = jnp.sum(my_terms[:, :, None] * powers[None], axis=1)
    keys = jnp.pad(keys, ((0, held * n - share), (0, 0)), constant_values=-1)
    keys = jnp.pad(keys.reshape(n, held, 8), ((0, 0), (0, width - held), (0, 0)), constant_values=-1)
    keys = keys.reshape(n * width, 8)
    points = jnp.pad(sample_points.T, ((0, PAD_INPUTS - INPUTS), (0, 0)))

    blocks = (n, FIELDS, width)
    vmem = pl.BlockSpec(memory_space=pltpu.VMEM)
    dma = pltpu.SemaphoreType.DMA
    f32 = jnp.float32
    coeffs, left = pl.pallas_call(
        functools.partial(fit_kernel, n, width, share, inverse_root),
        out_shape=(
            jax.ShapeDtypeStruct(blocks, f32),
            jax.ShapeDtypeStruct((FIELDS, rows), f32),
        ),
        in_specs=[vmem] * 5,
        out_specs=(vmem, vmem),
        scratch_shapes=[
            pltpu.VMEM((n * width, rows), jnp.bfloat16),
            *(pltpu.VMEM((table_width, rows), jnp.bfloat16) for _, table_width in GROUPS),
            *(pltpu.VMEM((count, FIELDS, width), f32) for count in (n, n // 2, n // 2, n) * 2),
            pltpu.VMEM((2, FIELDS, rows), f32),
            pltpu.VMEM((2, FIELDS, rows), f32),
            pltpu.VMEM((2, FIELDS, 128), f32),
            pltpu.VMEM((2, FIELDS, 128), f32),
            pltpu.VMEM((n, FIELDS, 128), f32),
            *(dma((2, n // 2)) for _ in range(6)), dma((2, n)),
            dma((2,)), dma((2,)), dma((2,)), dma((2,)),
            dma((n,)), dma((n,)),
        ],
        compiler_params=pltpu.CompilerParams(
            collective_id=0, has_side_effects=True, vmem_limit_bytes=48 * 1024 * 1024
        ),
    )(points, observed.T, keys, jnp.asarray(picks, jnp.bfloat16), jnp.asarray(entries))
    coeffs = coeffs.transpose(0, 2, 1)[:, :held, :].reshape(held * n, FIELDS)[:share]
    return coeffs, left.T


def solution(mesh):
    in_specs = (P(("groups", "samples"), None), P(("groups", "samples"), None), P())
    out_specs = (P(("groups", "terms"), None), P(("groups", "samples"), None))
    return jax.shard_map(
        per_device, mesh=mesh, in_specs=in_specs, out_specs=out_specs, check_vma=False
    )
```

```python
import functools
import itertools
import math

import jax
import jax.numpy as jnp
import numpy as np
from jax import lax
from jax.experimental import pallas as pl
from jax.experimental.pallas import tpu as pltpu
from jax.sharding import PartitionSpec as P

INPUTS = 10
DEGREE = 6
TERMS = 8008
FIELDS = 48
EPS = 1e-06
MESH = pl.DeviceIdType.MESH

GROUPS = (((0, 1, 2), 256), ((3, 4, 5), 256), ((6, 7), 128), ((8, 9), 128))
PAD_INPUTS = 16
PIECES = 3


def group_codes(count):
    return [c for c in itertools.product(range(DEGREE + 1), repeat=count) if sum(c) <= DEGREE]


def code_key(code):
    return sum(int(d) * (DEGREE + 1) ** i for i, d in enumerate(code))


def constants():
    depth = (DEGREE + 1) * PIECES * PAD_INPUTS
    blocks = []
    keys = np.full((8, 256), -2, np.int32)
    for g, (inputs, width) in enumerate(GROUPS):
        codes = group_codes(len(inputs)) * PIECES
        for r, code in enumerate(codes):
            keys[g, r] = code_key(code)
        for i, source in enumerate(inputs):
            block = np.zeros((width, depth), np.float32)
            for r, code in enumerate(codes):
                for piece in range(PIECES):
                    block[r, (code[i] * PIECES + piece) * PAD_INPUTS + source] = 1.0
            blocks.append(block)
    return np.concatenate(blocks), keys


def pieces_of(value):
    high = value.astype(jnp.bfloat16).astype(jnp.float32)
    rest = value - high
    middle = rest.astype(jnp.bfloat16).astype(jnp.float32)
    return high, middle, rest - middle


def fit_kernel(
    n, width, share, inverse_root,
    points_ref, observed_ref, index_ref, picks_ref, entries_ref,
    coeffs_ref, left_ref,
    design, keys_ref, t0, t1, t2, t3,
    send1, met1, recv1, all1, right1, send2, met2, recv2, all2, right2,
    cross_out, cross_in, small,
    pair_send, pair_recv, rs_send, rs_recv, ag_send, fw_send, ag_recv, cross_send, cross_recv, small_send, small_recv,
):
    me = lax.axis_index("samples")
    core = lax.axis_index("terms")
    rows = points_ref.shape[1]
    tables = (t0, t1, t2, t3)

    barrier = pltpu.get_barrier_semaphore()

    def greet(step, _):
        pl.semaphore_signal(
            barrier, inc=1, device_id={"samples": lax.rem(me + step, n), "terms": core}, device_id_type=MESH
        )
        return 0

    def greet_other(step, _):
        pl.semaphore_signal(
            barrier, inc=1, device_id={"samples": lax.rem(me + step, n), "terms": 1 - core}, device_id_type=MESH
        )
        return 0

    lax.fori_loop(1, n, greet, 0)
    lax.fori_loop(0, n, greet_other, 0)

    key_row = lax.broadcasted_iota(jnp.int32, keys_ref.shape, 0)
    keys = jnp.zeros(keys_ref.shape, jnp.int32)
    for g, (inputs, _) in enumerate(GROUPS):
        key = None
        for i, source in enumerate(inputs):
            part = index_ref[source:source + 1, :] * (DEGREE + 1) ** i
            key = part if key is None else key + part
        keys = jnp.where(key_row == g, key, keys)
    keys_ref[...] = keys.astype(jnp.float32)

    x = points_ref[...]
    values = [jnp.ones_like(x), x]
    for order in range(1, DEGREE):
        values.append(
            ((2 * order + 1) * x * values[order] - order * values[order - 1]) / (order + 1)
        )
    values = [v * np.float32(math.sqrt(2 * k + 1)) for k, v in enumerate(values)]
    parts = []
    for v in values:
        parts.extend(p.astype(jnp.bfloat16) for p in pieces_of(v))
    flat = jnp.concatenate(parts, axis=0)

    offset = 0
    for g, (inputs, table_width) in enumerate(GROUPS):
        table = None
        for _ in inputs:
            factor = jnp.dot(
                picks_ref[offset:offset + table_width, :], flat, preferred_element_type=jnp.float32
            )
            table = factor if table is None else table * factor
            offset += table_width
        count = len(group_codes(len(inputs)))
        row = lax.broadcasted_iota(jnp.int32, table.shape, 0)
        high, middle, low = pieces_of(table)
        tables[g][...] = jnp.where(
            row < count, high, jnp.where(row < 2 * count, middle, low)
        ).astype(jnp.bfloat16)

    squared = [v * v for v in values]
    poly = [squared[k][0:1, :] for k in range(DEGREE + 1)]
    for j in range(1, INPUTS):
        own = [squared[k][j:j + 1, :] for k in range(DEGREE + 1)]
        fresh = []
        for d in range(DEGREE + 1):
            total = poly[d] * own[0]
            for k in range(1, d + 1):
                total = total + poly[d - k] * own[k]
            fresh.append(total)
        poly = fresh
    squares = functools.reduce(lambda a, b: a + b, poly)
    weights = jnp.sqrt(TERMS / squares)
    row_scale = weights * np.float32(inverse_root)
    rhs = weights * observed_ref[...]

    def row_sums(value):
        return jnp.sum(value * value, axis=1, keepdims=True)

    def remote(src, dst, send_sem, recv_sem, peer):
        return pltpu.make_async_remote_copy(
            src_ref=src, dst_ref=dst, send_sem=send_sem, recv_sem=recv_sem,
            device_id=peer, device_id_type=MESH,
        )

    def small_copies(phase, step, terms):
        q = lax.rem(me + step, n)
        mine = core * n + me
        theirs = terms * n + q
        out = remote(
            small.at[phase, mine], small.at[phase, mine],
            small_send.at[phase, theirs], small_recv.at[phase, mine], {"samples": q, "terms": terms},
        )
        into = remote(
            small.at[phase, mine], small.at[phase, theirs],
            small_send.at[phase, theirs], small_recv.at[phase, theirs], {"samples": q, "terms": terms},
        )
        return out, into

    def tell(phase, column, both):
        small[phase, core * n + me] = jnp.broadcast_to(column, (FIELDS, 128)).T[0:8, :]

        def start(terms):
            def one(step, _):
                small_copies(phase, step, terms)[0].start()
                return 0
            return one

        lax.fori_loop(1, n, start(core), 0)
        if both:
            lax.fori_loop(0, n, start(1 - core), 0)

    def told(phase, both):
        def finish(terms):
            def one(step, _):
                out, into = small_copies(phase, step, terms)
                into.wait_recv()
                out.wait_send()
                return 0
            return one

        lax.fori_loop(1, n, finish(core), 0)
        first_slot, count = core * n, n
        if both:
            lax.fori_loop(0, n, finish(1 - core), 0)
            first_slot, count = 0, 2 * n
        total = lax.fori_loop(
            0, count, lambda i, acc: acc + small[phase, first_slot + i], jnp.zeros((8, FIELDS), jnp.float32)
        )
        return jnp.broadcast_to(total[0:1, :], (128, FIELDS)).T[:, 0:1]

    tile = min(width, 256)

    def build_chunk(q):
        def build_tile(i, _):
            at = pl.multiple_of(q * width + i * tile, tile)
            keys = keys_ref[:, pl.ds(at, tile)].T
            product = None
            for g, (_, table_width) in enumerate(GROUPS):
                hot = jnp.where(
                    keys[:, g:g + 1] == entries_ref[g:g + 1, 0:table_width], 1.0, 0.0
                ).astype(jnp.bfloat16)
                picked = jnp.dot(hot, tables[g][...], preferred_element_type=jnp.float32)
                product = picked if product is None else product * picked
            design[pl.ds(at, tile), :] = product.astype(jnp.bfloat16)
            return 0

        lax.fori_loop(0, width // tile, build_tile, 0)

    half = n // 2
    mine_h = me // 2
    mine_p = lax.rem(me, 2)
    across = 2 * mine_h + 1 - mine_p

    def transposed_all(left_rows, phase, send, met, recv, build):
        left_cast = left_rows.astype(jnp.bfloat16)

        def partial_chunk(q):
            if build:
                build_chunk(q)
            at = pl.multiple_of(q * width, width)
            return lax.dot_general(
                left_cast, design[pl.ds(at, width), :], (((1,), (1,)), ((), ())),
                preferred_element_type=jnp.float32,
            )

        def pair_copy(h):
            return remote(
                send.at[2 * h + 1 - mine_p], met.at[h],
                pair_send.at[phase, h], pair_recv.at[phase, h], {"samples": across},
            )

        def to_pair(step, _):
            h = lax.rem(mine_h + step, half)
            send[2 * h + 1 - mine_p] = partial_chunk(2 * h + 1 - mine_p)
            pair_copy(h).start()
            return 0

        lax.fori_loop(1, half + 1, to_pair, 0)

        def to_owner(step, _):
            h = lax.rem(mine_h + step, half)
            q = 2 * h + mine_p
            chunk = partial_chunk(q)
            pair_copy(h).wait_recv()
            chunk = chunk + met[h]

            @pl.when(step < half)
            def _():
                send[q] = chunk
                remote(
                    send.at[q], recv.at[mine_h], rs_send.at[phase, h], rs_recv.at[phase, mine_h], {"samples": q}
                ).start()

            @pl.when(step == half)
            def _():
                recv[mine_h] = chunk

            return 0

        lax.fori_loop(1, half + 1, to_owner, 0)

        def arrived(step, _):
            h = lax.rem(mine_h + step, half)
            q = 2 * h + mine_p
            copy = remote(
                send.at[q], recv.at[h], rs_send.at[phase, h], rs_recv.at[phase, h], {"samples": q}
            )
            copy.wait_recv()
            copy.wait_send()
            return 0

        def pair_sent(h, _):
            pair_copy(h).wait_send()
            return 0

        lax.fori_loop(1, half, arrived, 0)
        lax.fori_loop(0, half, pair_sent, 0)
        return lax.fori_loop(0, half, lambda h, acc: acc + recv[h], jnp.zeros((FIELDS, width), jnp.float32))

    def gather_product(raw, phase, blocks, rights):
        norm_phase = 2 * phase + 1
        blocks[me] = raw
        tell(norm_phase, row_sums(raw), True)

        def forward(h):
            q = 2 * h + mine_p
            return remote(
                blocks.at[q], blocks.at[q], fw_send.at[phase, h], ag_recv.at[phase, q], {"samples": across}
            )

        def spread(h, slot):
            return remote(
                blocks.at[me], blocks.at[slot], ag_send.at[phase, h], ag_recv.at[phase, slot],
                {"samples": 2 * h + mine_p},
            )

        def start(step, _):
            spread(lax.rem(mine_h + step, half), me).start()
            return 0

        forward(mine_h).start()
        lax.fori_loop(1, half, start, 0)
        alpha = jnp.sqrt(told(norm_phase, True) + EPS)

        def product(q, acc):
            right = blocks[q] / alpha
            rights[q] = right
            at = pl.multiple_of(q * width, width)
            return acc + jnp.dot(
                right.astype(jnp.bfloat16), design[pl.ds(at, width), :], preferred_element_type=jnp.float32
            )

        def hand_on(step, acc):
            h = lax.rem(mine_h + half - step, half)
            spread(h, 2 * h + mine_p).wait_recv()
            forward(h).start()
            return product(2 * h + mine_p, acc)

        def from_pair(step, acc):
            h = lax.rem(mine_h + half - step, half)
            q = 2 * h + 1 - mine_p
            remote(
                blocks.at[q], blocks.at[q], fw_send.at[phase, h], ag_recv.at[phase, q], {"samples": across}
            ).wait_recv()
            return product(q, acc)

        def sent(step, _):
            spread(lax.rem(mine_h + step, half), me).wait_send()
            return 0

        def forwarded(h, _):
            forward(h).wait_send()
            return 0

        acc = product(me, jnp.zeros((FIELDS, rows), jnp.float32))
        acc = lax.fori_loop(1, half, hand_on, acc)
        acc = lax.fori_loop(0, half, from_pair, acc)
        cross_out[phase] = acc
        copy = remote(
            cross_out.at[phase], cross_in.at[phase], cross_send.at[phase], cross_recv.at[phase], {"terms": 1 - core}
        )
        copy.start()
        lax.fori_loop(1, half, sent, 0)
        lax.fori_loop(0, half, forwarded, 0)
        copy.wait()
        return alpha, acc + cross_in[phase]

    pl.semaphore_wait(barrier, 2 * n - 1)
    tell(0, row_sums(rhs), False)
    summed = transposed_all(row_scale * rhs, 0, send1, met1, recv1, True)
    beta = jnp.sqrt(told(0, False) + EPS)
    left = rhs / beta
    alpha, image = gather_product(summed / beta, 0, all1, right1)
    phibar = beta
    rhobar = alpha

    partial = row_scale * image - alpha * left
    tell(2, row_sums(partial), False)
    summed = transposed_all(row_scale * partial, 1, send2, met2, recv2, False)
    beta = jnp.sqrt(told(2, False) + EPS)
    left = partial / beta
    alpha, image = gather_product(summed / beta - beta * right1[me], 1, all2, right2)
    rho = jnp.sqrt(rhobar * rhobar + beta * beta)
    cosine = rhobar / rho
    sine = beta / rho
    theta = sine * alpha
    rhobar = -cosine * alpha
    first = cosine * phibar / rho
    turn = theta / rho
    phibar = sine * phibar

    partial = row_scale * image - alpha * left
    tell(4, row_sums(partial), False)
    beta = jnp.sqrt(told(4, False) + EPS)
    left_ref[...] = partial / beta
    rho = jnp.sqrt(rhobar * rhobar + beta * beta)
    second = rhobar / rho * phibar / rho
    for q in range(-(-share // width)):
        at = q * width
        held = min(width, share - at)
        direction = right1[q][:, 0:held]
        coeffs_ref[:, at:at + held] = first * direction + second * (right2[q][:, 0:held] - turn * direction)


def per_device(sample_points, observed, multi_index):
    n = lax.axis_size("samples")
    cores = lax.axis_size("terms")
    rows = sample_points.shape[0]
    inverse_root = 1.0 / math.sqrt(rows * n)
    share = TERMS // cores
    width = -(-share // (n * 128)) * 128
    picks, entries = constants()

    my_terms = lax.dynamic_slice_in_dim(multi_index.T, lax.axis_index("terms") * share, share, 1)
    my_terms = jnp.pad(
        my_terms, ((0, PAD_INPUTS - INPUTS), (0, n * width - share)), constant_values=-1
    )
    points = jnp.pad(sample_points.T, ((0, PAD_INPUTS - INPUTS), (0, 0)))

    vmem = pl.BlockSpec(memory_space=pltpu.VMEM)
    dma = pltpu.SemaphoreType.DMA
    f32 = jnp.float32
    coeffs, left = pl.pallas_call(
        functools.partial(fit_kernel, n, width, share, inverse_root),
        out_shape=(
            jax.ShapeDtypeStruct((FIELDS, share), f32),
            jax.ShapeDtypeStruct((FIELDS, rows), f32),
        ),
        in_specs=[vmem] * 5,
        out_specs=(vmem, vmem),
        scratch_shapes=[
            pltpu.VMEM((n * width, rows), jnp.bfloat16),
            pltpu.VMEM((8, n * width), f32),
            *(pltpu.VMEM((table_width, rows), jnp.bfloat16) for _, table_width in GROUPS),
            *(pltpu.VMEM((count, FIELDS, width), f32) for count in (n, n // 2, n // 2, n, n) * 2),
            pltpu.VMEM((2, FIELDS, rows), f32),
            pltpu.VMEM((2, FIELDS, rows), f32),
            pltpu.VMEM((5, 2 * n, 8, FIELDS), f32),
            *(dma((2, n // 2)) for _ in range(6)), dma((2, n)), dma((2,)), dma((2,)),
            dma((5, 2 * n)), dma((5, 2 * n)),
        ],
        compiler_params=pltpu.CompilerParams(
            collective_id=0, has_side_effects=True, vmem_limit_bytes=48 * 1024 * 1024
        ),
    )(points, observed.T, my_terms, jnp.asarray(picks, jnp.bfloat16), jnp.asarray(entries, f32))
    return coeffs.T, left.T


def solution(mesh):
    in_specs = (P(("groups", "samples"), None), P(("groups", "samples"), None), P())
    out_specs = (P(("groups", "terms"), None), P(("groups", "samples"), None))
    return jax.shard_map(
        per_device, mesh=mesh, in_specs=in_specs, out_specs=out_specs, check_vma=False
    )
```

```python
import functools
import itertools
import math

import jax
import jax.numpy as jnp
import numpy as np
from jax import lax
from jax.experimental import pallas as pl
from jax.experimental.pallas import tpu as pltpu
from jax.sharding import PartitionSpec as P

INPUTS = 10
DEGREE = 6
TERMS = 8008
FIELDS = 48
EPS = 1e-06
MESH = pl.DeviceIdType.MESH

GROUPS = (((0, 1, 2), 256), ((3, 4, 5), 256), ((6, 7), 128), ((8, 9), 128))
PAD_INPUTS = 16
PIECES = 3


def group_codes(count):
    return [c for c in itertools.product(range(DEGREE + 1), repeat=count) if sum(c) <= DEGREE]


def code_key(code):
    return sum(int(d) * (DEGREE + 1) ** i for i, d in enumerate(code))


def constants():
    depth = (DEGREE + 1) * PIECES * PAD_INPUTS
    blocks = []
    keys = np.full((8, 256), -2, np.int32)
    for g, (inputs, width) in enumerate(GROUPS):
        codes = group_codes(len(inputs)) * PIECES
        for r, code in enumerate(codes):
            keys[g, r] = code_key(code)
        for i, source in enumerate(inputs):
            block = np.zeros((width, depth), np.float32)
            for r, code in enumerate(codes):
                for piece in range(PIECES):
                    block[r, (code[i] * PIECES + piece) * PAD_INPUTS + source] = 1.0
            blocks.append(block)
    return np.concatenate(blocks), keys


def pieces_of(value):
    high = value.astype(jnp.bfloat16).astype(jnp.float32)
    rest = value - high
    middle = rest.astype(jnp.bfloat16).astype(jnp.float32)
    return high, middle, rest - middle


def wrap(value, count):
    return jnp.where(value >= count, value - count, value)


def fit_kernel(
    n, width, share, inverse_root,
    points_ref, observed_hbm, index_ref, picks_hbm, entries_ref,
    coeffs_ref, left_ref,
    design, keys_ref, t0, t1, t2, t3,
    send1, met1, recv1, all1, right1, send2, met2, recv2, all2, right2,
    cross_out, cross_in, small,
    pair_send, pair_recv, rs_send, rs_recv, ag_send, fw_send, ag_recv, cross_send, cross_recv, small_send, small_recv, load_sem,
    observed_ref, picks_ref,
):
    me = lax.axis_index("samples")
    core = lax.axis_index("terms")
    rows = points_ref.shape[1]

    def each(first_step, stop, body, carry=0):
        return lax.fori_loop(first_step, stop, body, carry, unroll=n <= 8)

    tables = (t0, t1, t2, t3)

    load_picks = pltpu.make_async_copy(picks_hbm, picks_ref, load_sem.at[0])
    load_observed = pltpu.make_async_copy(observed_hbm, observed_ref, load_sem.at[1])
    load_picks.start()
    load_observed.start()

    barrier = pltpu.get_barrier_semaphore()

    def greet(step, _):
        pl.semaphore_signal(
            barrier, inc=1, device_id={"samples": wrap(me + step, n), "terms": core}, device_id_type=MESH
        )
        return 0

    each(1, n, greet, 0)
    pl.semaphore_signal(barrier, inc=1, device_id={"terms": 1 - core}, device_id_type=MESH)

    key_row = lax.broadcasted_iota(jnp.int32, keys_ref.shape, 0)
    keys = jnp.zeros(keys_ref.shape, jnp.int32)
    for g, (inputs, _) in enumerate(GROUPS):
        key = None
        for i, source in enumerate(inputs):
            part = index_ref[source:source + 1, :] * (DEGREE + 1) ** i
            key = part if key is None else key + part
        keys = jnp.where(key_row == g, key, keys)
    keys_ref[...] = keys.astype(jnp.float32)

    x = points_ref[...]
    values = [jnp.ones_like(x), x]
    for order in range(1, DEGREE):
        values.append(
            ((2 * order + 1) * x * values[order] - order * values[order - 1]) / (order + 1)
        )
    values = [v * np.float32(math.sqrt(2 * k + 1)) for k, v in enumerate(values)]
    parts = []
    for v in values:
        parts.extend(p.astype(jnp.bfloat16) for p in pieces_of(v))
    flat = jnp.concatenate(parts, axis=0)

    load_picks.wait()
    offset = 0
    for g, (inputs, table_width) in enumerate(GROUPS):
        table = None
        for _ in inputs:
            factor = jnp.dot(
                picks_ref[offset:offset + table_width, :], flat, preferred_element_type=jnp.float32
            )
            table = factor if table is None else table * factor
            offset += table_width
        count = len(group_codes(len(inputs)))
        row = lax.broadcasted_iota(jnp.int32, table.shape, 0)
        high, middle, low = pieces_of(table)
        tables[g][...] = jnp.where(
            row < count, high, jnp.where(row < 2 * count, middle, low)
        ).astype(jnp.bfloat16)

    squared = [v * v for v in values]
    poly = [squared[k][0:1, :] for k in range(DEGREE + 1)]
    for j in range(1, INPUTS):
        own = [squared[k][j:j + 1, :] for k in range(DEGREE + 1)]
        fresh = []
        for d in range(DEGREE + 1):
            total = poly[d] * own[0]
            for k in range(1, d + 1):
                total = total + poly[d - k] * own[k]
            fresh.append(total)
        poly = fresh
    squares = functools.reduce(lambda a, b: a + b, poly)
    weights = jnp.sqrt(TERMS / squares)
    row_scale = weights * np.float32(inverse_root)
    load_observed.wait()
    rhs = weights * observed_ref[...]

    def row_sums(value):
        return jnp.sum(value * value, axis=1, keepdims=True)

    def remote(src, dst, send_sem, recv_sem, peer):
        return pltpu.make_async_remote_copy(
            src_ref=src, dst_ref=dst, send_sem=send_sem, recv_sem=recv_sem,
            device_id=peer, device_id_type=MESH,
        )

    def small_copy(phase, step, slot):
        q = wrap(me + step, n)
        return remote(
            small.at[phase, me], small.at[phase, q if slot is None else slot],
            small_send.at[phase, q], small_recv.at[phase, q if slot is None else slot], {"samples": q},
        )

    def as_row(column):
        return jnp.broadcast_to(column, (FIELDS, 128)).T[0:8, :]

    def as_column(row):
        return jnp.broadcast_to(row[0:1, :], (128, FIELDS)).T[:, 0:1]

    def tell(phase, column):
        small[phase, me] = as_row(column)

        def start(step, _):
            small_copy(phase, step, me).start()
            return 0

        each(1, n, start)

    def told(phase, both):
        def arrive(step, _):
            small_copy(phase, step, None).wait_recv()
            return 0

        def leave(step, _):
            small_copy(phase, step, None).wait_send()
            return 0

        each(1, n, arrive)
        total = each(0, n, lambda i, acc: acc + small[phase, i], jnp.zeros((8, FIELDS), jnp.float32))
        if both:
            small[phase, n] = total
            copy = remote(
                small.at[phase, n], small.at[phase, n + 1],
                small_send.at[phase, n], small_recv.at[phase, n], {"terms": 1 - core},
            )
            copy.start()
            each(1, n, leave)
            copy.wait()
            total = total + small[phase, n + 1]
        else:
            each(1, n, leave)
        return as_column(total)

    tile = min(width, 512)

    def build_chunk(q):
        def build_tile(i, _):
            at = pl.multiple_of(q * width + i * tile, tile)
            keys = keys_ref[:, pl.ds(at, tile)].T
            product = None
            for g, (_, table_width) in enumerate(GROUPS):
                hot = jnp.where(
                    keys[:, g:g + 1] == entries_ref[g:g + 1, 0:table_width], 1.0, 0.0
                ).astype(jnp.bfloat16)
                picked = jnp.dot(hot, tables[g][...], preferred_element_type=jnp.float32)
                product = picked if product is None else product * picked
            design[pl.ds(at, tile), :] = product.astype(jnp.bfloat16)
            return 0

        lax.fori_loop(0, width // tile, build_tile, 0)

    half = n // 2
    mine_h = me // 2
    mine_p = lax.rem(me, 2)
    across = 2 * mine_h + 1 - mine_p

    def transposed_all(left_rows, phase, send, met, recv, build):
        left_cast = left_rows.astype(jnp.bfloat16)

        def partial_chunk(q):
            if build:
                build_chunk(q)
            at = pl.multiple_of(q * width, width)
            return lax.dot_general(
                left_cast, design[pl.ds(at, width), :], (((1,), (1,)), ((), ())),
                preferred_element_type=jnp.float32,
            )

        def pair_copy(h):
            return remote(
                send.at[2 * h + 1 - mine_p], met.at[h],
                pair_send.at[phase, h], pair_recv.at[phase, h], {"samples": across},
            )

        def to_pair(step, _):
            h = wrap(mine_h + step, half)
            send[2 * h + 1 - mine_p] = partial_chunk(2 * h + 1 - mine_p)
            pair_copy(h).start()
            return 0

        lax.fori_loop(1, half + 1, to_pair, 0)

        def to_owner(step, _):
            h = wrap(mine_h + step, half)
            q = 2 * h + mine_p
            chunk = partial_chunk(q)
            pair_copy(h).wait_recv()
            chunk = chunk + met[h]

            @pl.when(step < half)
            def _():
                send[q] = chunk
                remote(
                    send.at[q], recv.at[mine_h], rs_send.at[phase, h], rs_recv.at[phase, mine_h], {"samples": q}
                ).start()

            @pl.when(step == half)
            def _():
                recv[mine_h] = chunk

            return 0

        lax.fori_loop(1, half + 1, to_owner, 0)

        def arrived(step, _):
            h = wrap(mine_h + step, half)
            q = 2 * h + mine_p
            copy = remote(
                send.at[q], recv.at[h], rs_send.at[phase, h], rs_recv.at[phase, h], {"samples": q}
            )
            copy.wait_recv()
            copy.wait_send()
            return 0

        def pair_sent(h, _):
            pair_copy(h).wait_send()
            return 0

        each(1, half, arrived, 0)
        each(0, half, pair_sent, 0)
        return each(0, half, lambda h, acc: acc + recv[h], jnp.zeros((FIELDS, width), jnp.float32))

    def gather_product(raw, phase, blocks, rights):
        norm_phase = 2 * phase + 1
        blocks[me] = raw
        tell(norm_phase, row_sums(raw))

        def forward(h):
            q = 2 * h + mine_p
            return remote(
                blocks.at[q], blocks.at[q], fw_send.at[phase, h], ag_recv.at[phase, q], {"samples": across}
            )

        def spread(h, slot):
            return remote(
                blocks.at[me], blocks.at[slot], ag_send.at[phase, h], ag_recv.at[phase, slot],
                {"samples": 2 * h + mine_p},
            )

        def start(step, _):
            spread(wrap(mine_h + step, half), me).start()
            return 0

        forward(mine_h).start()
        each(1, half, start, 0)
        alpha = jnp.sqrt(told(norm_phase, True) + EPS)

        def product(q, acc):
            right = blocks[q] / alpha
            rights[q] = right
            at = pl.multiple_of(q * width, width)
            return acc + jnp.dot(
                right.astype(jnp.bfloat16), design[pl.ds(at, width), :], preferred_element_type=jnp.float32
            )

        def hand_on(step, acc):
            h = wrap(mine_h + half - step, half)
            spread(h, 2 * h + mine_p).wait_recv()
            forward(h).start()
            return product(2 * h + mine_p, acc)

        def from_pair(step, acc):
            h = wrap(mine_h + half - step, half)
            q = 2 * h + 1 - mine_p
            remote(
                blocks.at[q], blocks.at[q], fw_send.at[phase, h], ag_recv.at[phase, q], {"samples": across}
            ).wait_recv()
            return product(q, acc)

        def sent(step, _):
            spread(wrap(mine_h + step, half), me).wait_send()
            return 0

        def forwarded(h, _):
            forward(h).wait_send()
            return 0

        acc = product(me, jnp.zeros((FIELDS, rows), jnp.float32))
        acc = lax.fori_loop(1, half, hand_on, acc)
        acc = lax.fori_loop(0, half, from_pair, acc)
        cross_out[phase] = acc
        copy = remote(
            cross_out.at[phase], cross_in.at[phase], cross_send.at[phase], cross_recv.at[phase], {"terms": 1 - core}
        )
        copy.start()
        each(1, half, sent, 0)
        each(0, half, forwarded, 0)
        copy.wait()
        return alpha, acc + cross_in[phase]

    pl.semaphore_wait(barrier, n)
    tell(0, row_sums(rhs))
    summed = transposed_all(row_scale * rhs, 0, send1, met1, recv1, True)
    beta = jnp.sqrt(told(0, False) + EPS)
    left = rhs / beta
    alpha, image = gather_product(summed / beta, 0, all1, right1)
    phibar = beta
    rhobar = alpha

    partial = row_scale * image - alpha * left
    tell(2, row_sums(partial))
    summed = transposed_all(row_scale * partial, 1, send2, met2, recv2, False)
    beta = jnp.sqrt(told(2, False) + EPS)
    left = partial / beta
    alpha, image = gather_product(summed / beta - beta * right1[me], 1, all2, right2)
    rho = jnp.sqrt(rhobar * rhobar + beta * beta)
    cosine = rhobar / rho
    sine = beta / rho
    theta = sine * alpha
    rhobar = -cosine * alpha
    first = cosine * phibar / rho
    turn = theta / rho
    phibar = sine * phibar

    partial = row_scale * image - alpha * left
    tell(4, row_sums(partial))
    beta = jnp.sqrt(told(4, False) + EPS)
    left_ref[...] = partial / beta
    rho = jnp.sqrt(rhobar * rhobar + beta * beta)
    second = rhobar / rho * phibar / rho
    for q in range(-(-share // width)):
        at = q * width
        held = min(width, share - at)
        direction = right1[q][:, 0:held]
        coeffs_ref[:, at:at + held] = first * direction + second * (right2[q][:, 0:held] - turn * direction)


def per_device(sample_points, observed, multi_index):
    n = lax.axis_size("samples")
    cores = lax.axis_size("terms")
    rows = sample_points.shape[0]
    inverse_root = 1.0 / math.sqrt(rows * n)
    share = TERMS // cores
    width = -(-share // (n * 128)) * 128
    picks, entries = constants()

    my_terms = lax.dynamic_slice_in_dim(multi_index.T, lax.axis_index("terms") * share, share, 1)
    my_terms = jnp.pad(
        my_terms, ((0, PAD_INPUTS - INPUTS), (0, n * width - share)), constant_values=-1
    )
    points = jnp.pad(sample_points.T, ((0, PAD_INPUTS - INPUTS), (0, 0)))

    vmem = pl.BlockSpec(memory_space=pltpu.VMEM)
    dma = pltpu.SemaphoreType.DMA
    f32 = jnp.float32
    coeffs, left = pl.pallas_call(
        functools.partial(fit_kernel, n, width, share, inverse_root),
        out_shape=(
            jax.ShapeDtypeStruct((FIELDS, share), f32),
            jax.ShapeDtypeStruct((FIELDS, rows), f32),
        ),
        in_specs=[vmem, pl.BlockSpec(memory_space=pl.ANY), vmem, pl.BlockSpec(memory_space=pl.ANY), vmem],
        out_specs=(vmem, vmem),
        scratch_shapes=[
            pltpu.VMEM((n * width, rows), jnp.bfloat16),
            pltpu.VMEM((8, n * width), f32),
            *(pltpu.VMEM((table_width, rows), jnp.bfloat16) for _, table_width in GROUPS),
            *(pltpu.VMEM((count, FIELDS, width), f32) for count in (n, n // 2, n // 2, n, n) * 2),
            pltpu.VMEM((2, FIELDS, rows), f32),
            pltpu.VMEM((2, FIELDS, rows), f32),
            pltpu.VMEM((5, n + 2, 8, FIELDS), f32),
            *(dma((2, n // 2)) for _ in range(6)), dma((2, n)), dma((2,)), dma((2,)),
            dma((5, n + 1)), dma((5, n + 1)), dma((2,)),
            pltpu.VMEM((FIELDS, rows), f32),
            pltpu.VMEM(picks.shape, jnp.bfloat16),
        ],
        compiler_params=pltpu.CompilerParams(
            collective_id=0, has_side_effects=True, vmem_limit_bytes=56 * 1024 * 1024
        ),
    )(points, observed.T, my_terms, jnp.asarray(picks, jnp.bfloat16), jnp.asarray(entries, f32))
    return coeffs.T, left.T


def solution(mesh):
    in_specs = (P(("groups", "samples"), None), P(("groups", "samples"), None), P())
    out_specs = (P(("groups", "terms"), None), P(("groups", "samples"), None))
    return jax.shard_map(
        per_device, mesh=mesh, in_specs=in_specs, out_specs=out_specs, check_vma=False
    )
```

```python
import functools
import itertools
import math

import jax
import jax.numpy as jnp
import numpy as np
from jax import lax
from jax.experimental import pallas as pl
from jax.experimental.pallas import tpu as pltpu
from jax.sharding import PartitionSpec as P

INPUTS = 10
DEGREE = 6
TERMS = 8008
FIELDS = 48
EPS = 1e-06
MESH = pl.DeviceIdType.MESH

GROUPS = (((0, 1, 2), 256), ((3, 4, 5), 256), ((6, 7), 128), ((8, 9), 128))
PAD_INPUTS = 16
PIECES = 3


def group_codes(count):
    return [c for c in itertools.product(range(DEGREE + 1), repeat=count) if sum(c) <= DEGREE]


def code_key(code):
    return sum(int(d) * (DEGREE + 1) ** i for i, d in enumerate(code))


def constants():
    depth = (DEGREE + 1) * PIECES * PAD_INPUTS
    blocks = []
    keys = np.full((8, 256), -2, np.int32)
    for g, (inputs, width) in enumerate(GROUPS):
        codes = group_codes(len(inputs)) * PIECES
        for r, code in enumerate(codes):
            keys[g, r] = code_key(code)
        for i, source in enumerate(inputs):
            block = np.zeros((width, depth), np.float32)
            for r, code in enumerate(codes):
                for piece in range(PIECES):
                    block[r, (code[i] * PIECES + piece) * PAD_INPUTS + source] = 1.0
            blocks.append(block)
    return np.concatenate(blocks), keys


def pieces_of(value):
    high = value.astype(jnp.bfloat16).astype(jnp.float32)
    rest = value - high
    middle = rest.astype(jnp.bfloat16).astype(jnp.float32)
    return high, middle, rest - middle


def wrap(value, count):
    return jnp.where(value >= count, value - count, value)


def fit_kernel(
    n, width, share, inverse_root,
    points_ref, observed_hbm, index_ref, picks_hbm, entries_ref,
    coeffs_ref, left_ref,
    design, keys_ref, t0, t1, t2, t3,
    send1, met1, recv1, all1, right1, send2, met2, recv2, all2, right2,
    cross_out, cross_in, small,
    pair_send, pair_recv, rs_send, rs_recv, ag_send, fw_send, ag_recv, cross_send, cross_recv, small_send, small_recv, load_sem,
    observed_ref, picks_ref,
):
    me = lax.axis_index("samples")
    core = lax.axis_index("terms")
    rows = points_ref.shape[1]

    def each(first_step, stop, body, carry=0):
        return lax.fori_loop(first_step, stop, body, carry, unroll=n <= 8)

    tables = (t0, t1, t2, t3)

    load_picks = pltpu.make_async_copy(picks_hbm, picks_ref, load_sem.at[0])
    load_observed = pltpu.make_async_copy(observed_hbm, observed_ref, load_sem.at[1])
    load_picks.start()
    load_observed.start()

    barrier = pltpu.get_barrier_semaphore()

    def greet(step, _):
        pl.semaphore_signal(
            barrier, inc=1, device_id={"samples": wrap(me + step, n), "terms": core}, device_id_type=MESH
        )
        return 0

    each(1, n, greet, 0)
    pl.semaphore_signal(barrier, inc=1, device_id={"terms": 1 - core}, device_id_type=MESH)

    key_row = lax.broadcasted_iota(jnp.int32, keys_ref.shape, 0)
    keys = jnp.zeros(keys_ref.shape, jnp.int32)
    for g, (inputs, _) in enumerate(GROUPS):
        key = None
        for i, source in enumerate(inputs):
            part = index_ref[source:source + 1, :] * (DEGREE + 1) ** i
            key = part if key is None else key + part
        keys = jnp.where(key_row == g, key, keys)
    keys_ref[...] = keys.astype(jnp.float32)

    x = points_ref[...]
    values = [jnp.ones_like(x), x]
    for order in range(1, DEGREE):
        values.append(
            ((2 * order + 1) * x * values[order] - order * values[order - 1]) / (order + 1)
        )
    values = [v * np.float32(math.sqrt(2 * k + 1)) for k, v in enumerate(values)]
    parts = []
    for v in values:
        parts.extend(p.astype(jnp.bfloat16) for p in pieces_of(v))
    flat = jnp.concatenate(parts, axis=0)

    load_picks.wait()
    offset = 0
    for g, (inputs, table_width) in enumerate(GROUPS):
        table = None
        for _ in inputs:
            factor = jnp.dot(
                picks_ref[offset:offset + table_width, :], flat, preferred_element_type=jnp.float32
            )
            table = factor if table is None else table * factor
            offset += table_width
        count = len(group_codes(len(inputs)))
        row = lax.broadcasted_iota(jnp.int32, table.shape, 0)
        high, middle, low = pieces_of(table)
        tables[g][...] = jnp.where(
            row < count, high, jnp.where(row < 2 * count, middle, low)
        ).astype(jnp.bfloat16)

    squared = [v * v for v in values]
    poly = [squared[k][0:1, :] for k in range(DEGREE + 1)]
    for j in range(1, INPUTS):
        own = [squared[k][j:j + 1, :] for k in range(DEGREE + 1)]
        fresh = []
        for d in range(DEGREE + 1):
            total = poly[d] * own[0]
            for k in range(1, d + 1):
                total = total + poly[d - k] * own[k]
            fresh.append(total)
        poly = fresh
    squares = functools.reduce(lambda a, b: a + b, poly)
    weights = jnp.sqrt(TERMS / squares)
    row_scale = weights * np.float32(inverse_root)
    load_observed.wait()
    rhs = weights * observed_ref[...]

    def row_sums(value):
        return jnp.sum(value * value, axis=1, keepdims=True)

    def remote(src, dst, send_sem, recv_sem, peer):
        return pltpu.make_async_remote_copy(
            src_ref=src, dst_ref=dst, send_sem=send_sem, recv_sem=recv_sem,
            device_id=peer, device_id_type=MESH,
        )

    def small_copy(phase, step, slot):
        q = wrap(me + step, n)
        return remote(
            small.at[phase, me], small.at[phase, q if slot is None else slot],
            small_send.at[phase, q], small_recv.at[phase, q if slot is None else slot], {"samples": q},
        )

    def as_row(column):
        return jnp.broadcast_to(column, (FIELDS, 128)).T[0:8, :]

    def as_column(row):
        return jnp.broadcast_to(row[0:1, :], (128, FIELDS)).T[:, 0:1]

    def tell(phase, column):
        small[phase, me] = as_row(column)

        def start(step, _):
            small_copy(phase, step, me).start()
            return 0

        each(1, n, start)

    def told(phase, both):
        def arrive(step, _):
            small_copy(phase, step, None).wait_recv()
            return 0

        def leave(step, _):
            small_copy(phase, step, None).wait_send()
            return 0

        each(1, n, arrive)
        total = each(0, n, lambda i, acc: acc + small[phase, i], jnp.zeros((8, FIELDS), jnp.float32))
        if both:
            small[phase, n] = total
            copy = remote(
                small.at[phase, n], small.at[phase, n + 1],
                small_send.at[phase, n], small_recv.at[phase, n], {"terms": 1 - core},
            )
            copy.start()
            each(1, n, leave)
            copy.wait()
            total = total + small[phase, n + 1]
        else:
            each(1, n, leave)
        return as_column(total)

    tile = min(width, 512)

    def build_chunk(q):
        def build_tile(i, _):
            at = pl.multiple_of(q * width + i * tile, tile)
            keys = keys_ref[:, pl.ds(at, tile)].T
            product = None
            for g, (_, table_width) in enumerate(GROUPS):
                hot = jnp.where(
                    keys[:, g:g + 1] == entries_ref[g:g + 1, 0:table_width], 1.0, 0.0
                ).astype(jnp.bfloat16)
                picked = jnp.dot(hot, tables[g][...], preferred_element_type=jnp.float32)
                product = picked if product is None else product * picked
            design[pl.ds(at, tile), :] = product.astype(jnp.bfloat16)
            return 0

        lax.fori_loop(0, width // tile, build_tile, 0)

    half = n // 2
    mine_h = me // 2
    mine_p = lax.rem(me, 2)
    across = 2 * mine_h + 1 - mine_p

    def transposed_all(left_rows, phase, send, met, recv, build):
        left_cast = left_rows.T.astype(jnp.bfloat16)

        def partial_chunk(q):
            if build:
                build_chunk(q)
            at = pl.multiple_of(q * width, width)
            return jnp.dot(
                design[pl.ds(at, width), :], left_cast, preferred_element_type=jnp.float32
            ).T

        def pair_copy(h):
            return remote(
                send.at[2 * h + 1 - mine_p], met.at[h],
                pair_send.at[phase, h], pair_recv.at[phase, h], {"samples": across},
            )

        def to_pair(step, _):
            h = wrap(mine_h + step, half)
            send[2 * h + 1 - mine_p] = partial_chunk(2 * h + 1 - mine_p)
            pair_copy(h).start()
            return 0

        lax.fori_loop(1, half + 1, to_pair, 0)

        def to_owner(step, _):
            h = wrap(mine_h + step, half)
            q = 2 * h + mine_p
            chunk = partial_chunk(q)
            pair_copy(h).wait_recv()
            chunk = chunk + met[h]

            @pl.when(step < half)
            def _():
                send[q] = chunk
                remote(
                    send.at[q], recv.at[mine_h], rs_send.at[phase, h], rs_recv.at[phase, mine_h], {"samples": q}
                ).start()

            @pl.when(step == half)
            def _():
                recv[mine_h] = chunk

            return 0

        lax.fori_loop(1, half + 1, to_owner, 0)

        def arrived(step, _):
            h = wrap(mine_h + step, half)
            q = 2 * h + mine_p
            copy = remote(
                send.at[q], recv.at[h], rs_send.at[phase, h], rs_recv.at[phase, h], {"samples": q}
            )
            copy.wait_recv()
            copy.wait_send()
            return 0

        def pair_sent(h, _):
            pair_copy(h).wait_send()
            return 0

        each(1, half, arrived, 0)
        each(0, half, pair_sent, 0)
        return each(0, half, lambda h, acc: acc + recv[h], jnp.zeros((FIELDS, width), jnp.float32))

    def gather_product(raw, phase, blocks, rights):
        norm_phase = 2 * phase + 1
        blocks[me] = raw
        tell(norm_phase, row_sums(raw))

        def forward(h):
            q = 2 * h + mine_p
            return remote(
                blocks.at[q], blocks.at[q], fw_send.at[phase, h], ag_recv.at[phase, q], {"samples": across}
            )

        def spread(h, slot):
            return remote(
                blocks.at[me], blocks.at[slot], ag_send.at[phase, h], ag_recv.at[phase, slot],
                {"samples": 2 * h + mine_p},
            )

        def start(step, _):
            spread(wrap(mine_h + step, half), me).start()
            return 0

        forward(mine_h).start()
        each(1, half, start, 0)
        alpha = jnp.sqrt(told(norm_phase, True) + EPS)

        def product(q, acc):
            right = blocks[q] / alpha
            rights[q] = right
            at = pl.multiple_of(q * width, width)
            return acc + jnp.dot(
                right.astype(jnp.bfloat16), design[pl.ds(at, width), :], preferred_element_type=jnp.float32
            )

        def hand_on(step, acc):
            h = wrap(mine_h + half - step, half)
            spread(h, 2 * h + mine_p).wait_recv()
            forward(h).start()
            return product(2 * h + mine_p, acc)

        def from_pair(step, acc):
            h = wrap(mine_h + half - step, half)
            q = 2 * h + 1 - mine_p
            remote(
                blocks.at[q], blocks.at[q], fw_send.at[phase, h], ag_recv.at[phase, q], {"samples": across}
            ).wait_recv()
            return product(q, acc)

        def sent(step, _):
            spread(wrap(mine_h + step, half), me).wait_send()
            return 0

        def forwarded(h, _):
            forward(h).wait_send()
            return 0

        acc = product(me, jnp.zeros((FIELDS, rows), jnp.float32))
        acc = lax.fori_loop(1, half, hand_on, acc)
        acc = lax.fori_loop(0, half, from_pair, acc)
        cross_out[phase] = acc
        copy = remote(
            cross_out.at[phase], cross_in.at[phase], cross_send.at[phase], cross_recv.at[phase], {"terms": 1 - core}
        )
        copy.start()
        each(1, half, sent, 0)
        each(0, half, forwarded, 0)
        copy.wait()
        return alpha, acc + cross_in[phase]

    pl.semaphore_wait(barrier, n)
    tell(0, row_sums(rhs))
    summed = transposed_all(row_scale * rhs, 0, send1, met1, recv1, True)
    beta = jnp.sqrt(told(0, False) + EPS)
    left = rhs / beta
    alpha, image = gather_product(summed / beta, 0, all1, right1)
    phibar = beta
    rhobar = alpha

    partial = row_scale * image - alpha * left
    tell(2, row_sums(partial))
    summed = transposed_all(row_scale * partial, 1, send2, met2, recv2, False)
    beta = jnp.sqrt(told(2, False) + EPS)
    left = partial / beta
    alpha, image = gather_product(summed / beta - beta * right1[me], 1, all2, right2)
    rho = jnp.sqrt(rhobar * rhobar + beta * beta)
    cosine = rhobar / rho
    sine = beta / rho
    theta = sine * alpha
    rhobar = -cosine * alpha
    first = cosine * phibar / rho
    turn = theta / rho
    phibar = sine * phibar

    partial = row_scale * image - alpha * left
    tell(4, row_sums(partial))
    beta = jnp.sqrt(told(4, False) + EPS)
    left_ref[...] = partial / beta
    rho = jnp.sqrt(rhobar * rhobar + beta * beta)
    second = rhobar / rho * phibar / rho
    for q in range(-(-share // width)):
        at = q * width
        held = min(width, share - at)
        direction = right1[q][:, 0:held]
        coeffs_ref[:, at:at + held] = first * direction + second * (right2[q][:, 0:held] - turn * direction)


def per_device(sample_points, observed, multi_index):
    n = lax.axis_size("samples")
    cores = lax.axis_size("terms")
    rows = sample_points.shape[0]
    inverse_root = 1.0 / math.sqrt(rows * n)
    share = TERMS // cores
    width = -(-share // (n * 128)) * 128
    picks, entries = constants()

    my_terms = lax.dynamic_slice_in_dim(multi_index.T, lax.axis_index("terms") * share, share, 1)
    my_terms = jnp.pad(
        my_terms, ((0, PAD_INPUTS - INPUTS), (0, n * width - share)), constant_values=-1
    )
    points = jnp.pad(sample_points.T, ((0, PAD_INPUTS - INPUTS), (0, 0)))

    vmem = pl.BlockSpec(memory_space=pltpu.VMEM)
    dma = pltpu.SemaphoreType.DMA
    f32 = jnp.float32
    coeffs, left = pl.pallas_call(
        functools.partial(fit_kernel, n, width, share, inverse_root),
        out_shape=(
            jax.ShapeDtypeStruct((FIELDS, share), f32),
            jax.ShapeDtypeStruct((FIELDS, rows), f32),
        ),
        in_specs=[vmem, pl.BlockSpec(memory_space=pl.ANY), vmem, pl.BlockSpec(memory_space=pl.ANY), vmem],
        out_specs=(vmem, vmem),
        scratch_shapes=[
            pltpu.VMEM((n * width, rows), jnp.bfloat16),
            pltpu.VMEM((8, n * width), f32),
            *(pltpu.VMEM((table_width, rows), jnp.bfloat16) for _, table_width in GROUPS),
            *(pltpu.VMEM((count, FIELDS, width), f32) for count in (n, n // 2, n // 2, n, n) * 2),
            pltpu.VMEM((2, FIELDS, rows), f32),
            pltpu.VMEM((2, FIELDS, rows), f32),
            pltpu.VMEM((5, n + 2, 8, FIELDS), f32),
            *(dma((2, n // 2)) for _ in range(6)), dma((2, n)), dma((2,)), dma((2,)),
            dma((5, n + 1)), dma((5, n + 1)), dma((2,)),
            pltpu.VMEM((FIELDS, rows), f32),
            pltpu.VMEM(picks.shape, jnp.bfloat16),
        ],
        compiler_params=pltpu.CompilerParams(
            collective_id=0, has_side_effects=True, vmem_limit_bytes=44 * 1024 * 1024
        ),
    )(points, observed.T, my_terms, jnp.asarray(picks, jnp.bfloat16), jnp.asarray(entries, f32))
    return coeffs.T, left.T


def solution(mesh):
    in_specs = (P(("groups", "samples"), None), P(("groups", "samples"), None), P())
    out_specs = (P(("groups", "terms"), None), P(("groups", "samples"), None))
    return jax.shard_map(
        per_device, mesh=mesh, in_specs=in_specs, out_specs=out_specs, check_vma=False
    )
```

```python
import functools
import itertools
import math

import jax
import jax.numpy as jnp
import numpy as np
from jax import lax
from jax.experimental import pallas as pl
from jax.experimental.pallas import tpu as pltpu
from jax.sharding import PartitionSpec as P

INPUTS = 10
DEGREE = 6
TERMS = 8008
FIELDS = 48
EPS = 1e-06
MESH = pl.DeviceIdType.MESH

GROUPS = (((0, 1, 2), 256), ((3, 4, 5), 256), ((6, 7), 128), ((8, 9), 128))
PAD_INPUTS = 16
PIECES = 3


def group_codes(count):
    return [c for c in itertools.product(range(DEGREE + 1), repeat=count) if sum(c) <= DEGREE]


def code_key(code):
    return sum(int(d) * (DEGREE + 1) ** i for i, d in enumerate(code))


def constants():
    depth = (DEGREE + 1) * PIECES * PAD_INPUTS
    blocks = []
    keys = np.full((8, 256), -2, np.int32)
    for g, (inputs, width) in enumerate(GROUPS):
        codes = group_codes(len(inputs)) * PIECES
        for r, code in enumerate(codes):
            keys[g, r] = code_key(code)
        for i, source in enumerate(inputs):
            block = np.zeros((width, depth), np.float32)
            for r, code in enumerate(codes):
                for piece in range(PIECES):
                    block[r, (code[i] * PIECES + piece) * PAD_INPUTS + source] = 1.0
            blocks.append(block)
    return np.concatenate(blocks), keys


def pieces_of(value):
    high = value.astype(jnp.bfloat16).astype(jnp.float32)
    rest = value - high
    middle = rest.astype(jnp.bfloat16).astype(jnp.float32)
    return high, middle, rest - middle


def wrap(value, count):
    return jnp.where(value >= count, value - count, value)


def fit_kernel(
    n, width, share, inverse_root,
    points_ref, observed_hbm, index_ref, picks_hbm, entries_ref,
    coeffs_ref, left_ref,
    design, keys_ref, t0, t1, t2, t3,
    send1, met1, recv1, all1, right1, send2, met2, recv2, all2, right2,
    cross_out, cross_in, small,
    pair_send, pair_recv, rs_send, rs_recv, ag_send, fw_send, ag_recv, cross_send, cross_recv, small_send, small_recv, load_sem,
    observed_ref, picks_ref,
):
    me = lax.axis_index("samples")
    core = lax.axis_index("terms")
    rows = points_ref.shape[1]

    def each(first_step, stop, body, carry=0):
        return lax.fori_loop(first_step, stop, body, carry, unroll=n <= 8)

    tables = (t0, t1, t2, t3)

    load_picks = pltpu.make_async_copy(picks_hbm, picks_ref, load_sem.at[0])
    load_observed = pltpu.make_async_copy(observed_hbm, observed_ref, load_sem.at[1])
    load_picks.start()
    load_observed.start()

    barrier = pltpu.get_barrier_semaphore()

    def greet(step, _):
        pl.semaphore_signal(
            barrier, inc=1, device_id={"samples": wrap(me + step, n), "terms": core}, device_id_type=MESH
        )
        return 0

    each(1, n, greet, 0)
    pl.semaphore_signal(barrier, inc=1, device_id={"terms": 1 - core}, device_id_type=MESH)

    key_row = lax.broadcasted_iota(jnp.int32, keys_ref.shape, 0)
    keys = jnp.zeros(keys_ref.shape, jnp.int32)
    for g, (inputs, _) in enumerate(GROUPS):
        key = None
        for i, source in enumerate(inputs):
            part = index_ref[source:source + 1, :] * (DEGREE + 1) ** i
            key = part if key is None else key + part
        keys = jnp.where(key_row == g, key, keys)
    keys_ref[...] = keys.astype(jnp.float32)

    x = points_ref[...]
    values = [jnp.ones_like(x), x]
    for order in range(1, DEGREE):
        values.append(
            ((2 * order + 1) * x * values[order] - order * values[order - 1]) / (order + 1)
        )
    values = [v * np.float32(math.sqrt(2 * k + 1)) for k, v in enumerate(values)]
    parts = []
    for v in values:
        parts.extend(p.astype(jnp.bfloat16) for p in pieces_of(v))
    flat = jnp.concatenate(parts, axis=0)

    load_picks.wait()
    offset = 0
    for g, (inputs, table_width) in enumerate(GROUPS):
        table = None
        for _ in inputs:
            factor = jnp.dot(
                picks_ref[offset:offset + table_width, :], flat, preferred_element_type=jnp.float32
            )
            table = factor if table is None else table * factor
            offset += table_width
        count = len(group_codes(len(inputs)))
        row = lax.broadcasted_iota(jnp.int32, table.shape, 0)
        high, middle, low = pieces_of(table)
        tables[g][...] = jnp.where(
            row < count, high, jnp.where(row < 2 * count, middle, low)
        ).astype(jnp.bfloat16)

    squared = [v * v for v in values]
    poly = [squared[k][0:1, :] for k in range(DEGREE + 1)]
    for j in range(1, INPUTS):
        own = [squared[k][j:j + 1, :] for k in range(DEGREE + 1)]
        fresh = []
        for d in range(DEGREE + 1):
            total = poly[d] * own[0]
            for k in range(1, d + 1):
                total = total + poly[d - k] * own[k]
            fresh.append(total)
        poly = fresh
    squares = functools.reduce(lambda a, b: a + b, poly)
    weights = jnp.sqrt(TERMS / squares)
    row_scale = weights * np.float32(inverse_root)
    load_observed.wait()
    rhs = weights * observed_ref[...]

    def row_sums(value):
        return jnp.sum(value * value, axis=1, keepdims=True)

    def remote(src, dst, send_sem, recv_sem, peer):
        return pltpu.make_async_remote_copy(
            src_ref=src, dst_ref=dst, send_sem=send_sem, recv_sem=recv_sem,
            device_id=peer, device_id_type=MESH,
        )

    def small_copy(phase, step, slot):
        q = wrap(me + step, n)
        return remote(
            small.at[phase, me], small.at[phase, q if slot is None else slot],
            small_send.at[phase, q], small_recv.at[phase, q if slot is None else slot], {"samples": q},
        )

    def as_row(column):
        return jnp.broadcast_to(column, (FIELDS, 128)).T[0:8, :]

    def as_column(row):
        return jnp.broadcast_to(row[0:1, :], (128, FIELDS)).T[:, 0:1]

    def tell(phase, column):
        small[phase, me] = as_row(column)

        def start(step, _):
            small_copy(phase, step, me).start()
            return 0

        each(1, n, start)

    def told(phase, both):
        def arrive(step, _):
            small_copy(phase, step, None).wait_recv()
            return 0

        def leave(step, _):
            small_copy(phase, step, None).wait_send()
            return 0

        each(1, n, arrive)
        total = each(0, n, lambda i, acc: acc + small[phase, i], jnp.zeros((8, FIELDS), jnp.float32))
        if both:
            small[phase, n] = total
            copy = remote(
                small.at[phase, n], small.at[phase, n + 1],
                small_send.at[phase, n], small_recv.at[phase, n], {"terms": 1 - core},
            )
            copy.start()
            each(1, n, leave)
            copy.wait()
            total = total + small[phase, n + 1]
        else:
            each(1, n, leave)
        return as_column(total)

    tile = min(width, 512)

    def build_chunk(q):
        def build_tile(i, _):
            at = pl.multiple_of(q * width + i * tile, tile)
            keys = keys_ref[:, pl.ds(at, tile)].T
            product = None
            for g, (_, table_width) in enumerate(GROUPS):
                hot = jnp.where(
                    keys[:, g:g + 1] == entries_ref[g:g + 1, 0:table_width], 1.0, 0.0
                ).astype(jnp.bfloat16)
                picked = jnp.dot(hot, tables[g][...], preferred_element_type=jnp.float32)
                product = picked if product is None else product * picked
            design[pl.ds(at, tile), :] = product.astype(jnp.bfloat16)
            return 0

        lax.fori_loop(0, width // tile, build_tile, 0)

    half = n // 2
    mine_h = me // 2
    mine_p = lax.rem(me, 2)
    across = 2 * mine_h + 1 - mine_p

    def transposed_all(left_rows, phase, send, met, recv, build):
        left_cast = left_rows.T.astype(jnp.bfloat16)

        def partial_chunk(q):
            if build:
                build_chunk(q)
            at = pl.multiple_of(q * width, width)
            return jnp.dot(
                design[pl.ds(at, width), :], left_cast, preferred_element_type=jnp.float32
            ).T

        def pair_copy(h):
            return remote(
                send.at[2 * h + 1 - mine_p], met.at[h],
                pair_send.at[phase, h], pair_recv.at[phase, h], {"samples": across},
            )

        def to_pair(step, _):
            h = wrap(mine_h + step, half)
            send[2 * h + 1 - mine_p] = partial_chunk(2 * h + 1 - mine_p)
            pair_copy(h).start()
            return 0

        lax.fori_loop(1, half + 1, to_pair, 0)

        def to_owner(step, _):
            h = wrap(mine_h + step, half)
            q = 2 * h + mine_p
            chunk = partial_chunk(q)
            pair_copy(h).wait_recv()
            chunk = chunk + met[h]

            @pl.when(step < half)
            def _():
                send[q] = chunk
                remote(
                    send.at[q], recv.at[mine_h], rs_send.at[phase, h], rs_recv.at[phase, mine_h], {"samples": q}
                ).start()

            @pl.when(step == half)
            def _():
                recv[mine_h] = chunk

            return 0

        lax.fori_loop(1, half + 1, to_owner, 0)

        def arrived(step, _):
            h = wrap(mine_h + step, half)
            q = 2 * h + mine_p
            copy = remote(
                send.at[q], recv.at[h], rs_send.at[phase, h], rs_recv.at[phase, h], {"samples": q}
            )
            copy.wait_recv()
            copy.wait_send()
            return 0

        def pair_sent(h, _):
            pair_copy(h).wait_send()
            return 0

        each(1, half, arrived, 0)
        each(0, half, pair_sent, 0)
        return each(0, half, lambda h, acc: acc + recv[h], jnp.zeros((FIELDS, width), jnp.float32))

    def gather_product(raw, phase, blocks, rights):
        norm_phase = 2 * phase + 1
        blocks[me] = raw
        tell(norm_phase, row_sums(raw))

        def forward(h):
            q = 2 * h + mine_p
            return remote(
                blocks.at[q], blocks.at[q], fw_send.at[phase, h], ag_recv.at[phase, q], {"samples": across}
            )

        def spread(h, slot):
            return remote(
                blocks.at[me], blocks.at[slot], ag_send.at[phase, h], ag_recv.at[phase, slot],
                {"samples": 2 * h + mine_p},
            )

        def start(step, _):
            spread(wrap(mine_h + step, half), me).start()
            return 0

        forward(mine_h).start()
        each(1, half, start, 0)

        def along(step):
            h = wrap(mine_h + half - step, half)
            return h, 2 * h + mine_p

        def pass_on(step):
            h, q = along(step)
            spread(h, q).wait_recv()
            forward(h).start()

        pass_on(1)
        alpha = jnp.sqrt(told(norm_phase, True) + EPS)

        def product(q, acc):
            right = blocks[q] / alpha
            rights[q] = right
            at = pl.multiple_of(q * width, width)
            return acc + jnp.dot(
                right.astype(jnp.bfloat16), design[pl.ds(at, width), :], preferred_element_type=jnp.float32
            )

        def hand_on(step, acc):
            pass_on(step)
            return product(along(step - 1)[1], acc)

        def from_pair(step, acc):
            h = wrap(mine_h + half - step, half)
            q = 2 * h + 1 - mine_p
            remote(
                blocks.at[q], blocks.at[q], fw_send.at[phase, h], ag_recv.at[phase, q], {"samples": across}
            ).wait_recv()
            return product(q, acc)

        def sent(step, _):
            spread(wrap(mine_h + step, half), me).wait_send()
            return 0

        def forwarded(h, _):
            forward(h).wait_send()
            return 0

        acc = product(me, jnp.zeros((FIELDS, rows), jnp.float32))
        acc = lax.fori_loop(2, half, hand_on, acc)
        acc = product(along(half - 1)[1], acc)
        acc = lax.fori_loop(0, half, from_pair, acc)
        cross_out[phase] = acc
        copy = remote(
            cross_out.at[phase], cross_in.at[phase], cross_send.at[phase], cross_recv.at[phase], {"terms": 1 - core}
        )
        copy.start()
        each(1, half, sent, 0)
        each(0, half, forwarded, 0)
        copy.wait()
        return alpha, acc + cross_in[phase]

    pl.semaphore_wait(barrier, n)
    tell(0, row_sums(rhs))
    summed = transposed_all(row_scale * rhs, 0, send1, met1, recv1, True)
    beta = jnp.sqrt(told(0, False) + EPS)
    left = rhs / beta
    alpha, image = gather_product(summed / beta, 0, all1, right1)
    phibar = beta
    rhobar = alpha

    partial = row_scale * image - alpha * left
    tell(2, row_sums(partial))
    summed = transposed_all(row_scale * partial, 1, send2, met2, recv2, False)
    beta = jnp.sqrt(told(2, False) + EPS)
    left = partial / beta
    alpha, image = gather_product(summed / beta - beta * right1[me], 1, all2, right2)
    rho = jnp.sqrt(rhobar * rhobar + beta * beta)
    cosine = rhobar / rho
    sine = beta / rho
    theta = sine * alpha
    rhobar = -cosine * alpha
    first = cosine * phibar / rho
    turn = theta / rho
    phibar = sine * phibar

    partial = row_scale * image - alpha * left
    tell(4, row_sums(partial))
    beta = jnp.sqrt(told(4, False) + EPS)
    left_ref[...] = partial / beta
    rho = jnp.sqrt(rhobar * rhobar + beta * beta)
    second = rhobar / rho * phibar / rho
    for q in range(-(-share // width)):
        at = q * width
        held = min(width, share - at)
        direction = right1[q][:, 0:held]
        coeffs_ref[:, at:at + held] = first * direction + second * (right2[q][:, 0:held] - turn * direction)


def per_device(sample_points, observed, multi_index):
    n = lax.axis_size("samples")
    cores = lax.axis_size("terms")
    rows = sample_points.shape[0]
    inverse_root = 1.0 / math.sqrt(rows * n)
    share = TERMS // cores
    width = -(-share // (n * 128)) * 128
    picks, entries = constants()

    my_terms = lax.dynamic_slice_in_dim(multi_index.T, lax.axis_index("terms") * share, share, 1)
    my_terms = jnp.pad(
        my_terms, ((0, PAD_INPUTS - INPUTS), (0, n * width - share)), constant_values=-1
    )
    points = jnp.pad(sample_points.T, ((0, PAD_INPUTS - INPUTS), (0, 0)))

    vmem = pl.BlockSpec(memory_space=pltpu.VMEM)
    dma = pltpu.SemaphoreType.DMA
    f32 = jnp.float32
    coeffs, left = pl.pallas_call(
        functools.partial(fit_kernel, n, width, share, inverse_root),
        out_shape=(
            jax.ShapeDtypeStruct((FIELDS, share), f32),
            jax.ShapeDtypeStruct((FIELDS, rows), f32),
        ),
        in_specs=[vmem, pl.BlockSpec(memory_space=pl.ANY), vmem, pl.BlockSpec(memory_space=pl.ANY), vmem],
        out_specs=(vmem, vmem),
        scratch_shapes=[
            pltpu.VMEM((n * width, rows), jnp.bfloat16),
            pltpu.VMEM((8, n * width), f32),
            *(pltpu.VMEM((table_width, rows), jnp.bfloat16) for _, table_width in GROUPS),
            *(pltpu.VMEM((count, FIELDS, width), f32) for count in (n, n // 2, n // 2, n, n) * 2),
            pltpu.VMEM((2, FIELDS, rows), f32),
            pltpu.VMEM((2, FIELDS, rows), f32),
            pltpu.VMEM((5, n + 2, 8, FIELDS), f32),
            *(dma((2, n // 2)) for _ in range(6)), dma((2, n)), dma((2,)), dma((2,)),
            dma((5, n + 1)), dma((5, n + 1)), dma((2,)),
            pltpu.VMEM((FIELDS, rows), f32),
            pltpu.VMEM(picks.shape, jnp.bfloat16),
        ],
        compiler_params=pltpu.CompilerParams(
            collective_id=0, has_side_effects=True, vmem_limit_bytes=56 * 1024 * 1024
        ),
    )(points, observed.T, my_terms, jnp.asarray(picks, jnp.bfloat16), jnp.asarray(entries, f32))
    return coeffs.T, left.T


def solution(mesh):
    in_specs = (P(("groups", "samples"), None), P(("groups", "samples"), None), P())
    out_specs = (P(("groups", "terms"), None), P(("groups", "samples"), None))
    return jax.shard_map(
        per_device, mesh=mesh, in_specs=in_specs, out_specs=out_specs, check_vma=False
    )
```
